32 devices in a mesh: items: 8 (over z, x), ffn: 4 (over y, core).
Axes of the slice: x: 2, y: 2, z: 4, core: 2. Of those that a mesh axis runs over, the one named last changes fastest.
Arguments:
- text_rows: bfloat16 [32, 4, 502, 768], P(('items', 'ffn')), may hold values from -6 to 6
- attn_weight: bfloat16 [3072, 768], P(('items', 'ffn'))
- vectors: bfloat16 [18, 768], P(None, ('items', 'ffn'))
- w_in: bfloat16 [768, 3072], P('items', 'ffn'), may hold values from -0.21875 to 0.21875
- b_in: bfloat16 [4, 768], P('ffn', 'items'), may hold values from -1.5 to 1.5
- w_out: bfloat16 [3072, 768], P('ffn', 'items'), may hold values from -0.109375 to 0.109375
- seg_count: int32 [32], P(('items', 'ffn')), may hold values from 2 to 4, as said below
- last_fill: int32 [32], P(('items', 'ffn')), may hold values from 1 to 502, as said below
- out_grad: bfloat16 [32, 4, 502, 768], P(('items', 'ffn')), may hold values from -6 to 6
- mem_grad: float32 [32, 10, 768], P(('items', 'ffn')), may hold values from -6 to 6
Outputs:
- activations: bfloat16 [32, 4, 502, 768], P(('items', 'ffn'))
- final_memory: float32 [32, 10, 768], P(('items', 'ffn'))
- text_grad: float32 [32, 4, 502, 768], P(('items', 'ffn'))
- attn_grad: float32 [3072, 768], P(('items', 'ffn'))
- vector_grad: float32 [18, 768], P(None, ('items', 'ffn'))
- w_in_grad: float32 [768, 3072], P('items', 'ffn')
- b_in_grad: float32 [4, 768], P('ffn', 'items')
- w_out_grad: float32 [3072, 768], P('ffn', 'items')
The draws below stay inside these ranges and needn't reach their ends.
Inputs may be any that keep to these rules, and one draw needn't show every extreme that they name: `seg_count`: some item has 4 segments. `last_fill`: some item's last segment is full.
All inputs are finite; a program needn't handle non-finite values.
Results may differ from the reference program's by a relative error of at most 0.025.
Values may be sent and summed in bfloat16 or wider, within the bound.
No kernel may reach another device: no remote copies, remote signals or barrier semaphores. Data moves between devices by JAX's collectives and lax.ppermute only.
A program may use at most 384 MiB of HBM per device.

```python
import jax
import jax.numpy as jnp
from jax import lax

HEADS = 12
HD = 64
D = 768
FF = 3072
MEM = 10
TEXT = 502
SEGS_MAX = 4
ITEMS = 32
N_FFN = 4


def unit_noise(key, shape):
    return jax.random.normal(key, shape, jnp.float32)


def draw_attn_weight(key, part):
    key = jax.random.fold_in(key, 11)
    noise = unit_noise(key, (4 * D, D))
    row_index = jnp.arange(4 * D)
    out_scale = (2.0 * D / (TEXT + 2 * MEM)) ** (-0.5)
    factor = jnp.where(row_index < 3 * D, D ** (-0.5), out_scale)
    return (noise * factor[:, None]).astype(jnp.bfloat16)


def draw_vectors(key, part):
    key = jax.random.fold_in(key, 12)
    noise = unit_noise(key, (8 + MEM, D))
    row_index = jnp.arange(8 + MEM)[:, None]
    is_gain = (row_index == 3) | (row_index == 6)
    factor = jnp.where(row_index >= 8, 1.0, 0.3)
    return (jnp.where(is_gain, 1.0, 0.0) + factor * noise).astype(jnp.bfloat16)


def draw_seg_count(key, part):
    key = jax.random.fold_in(key, 13)
    first_key, second_key = jax.random.split(key)
    counts = jax.random.randint(first_key, (ITEMS,), 2, SEGS_MAX + 1)
    chosen = jax.random.randint(second_key, (), 0, ITEMS)
    return jnp.where(jnp.arange(ITEMS) == chosen, SEGS_MAX, counts).astype(jnp.int32)


def draw_last_fill(key, part):
    key = jax.random.fold_in(key, 14)
    first_key, second_key = jax.random.split(key)
    fills = jax.random.randint(first_key, (ITEMS,), 1, TEXT + 1)
    chosen = jax.random.randint(second_key, (), 0, ITEMS)
    return jnp.where(jnp.arange(ITEMS) == chosen, TEXT, fills).astype(jnp.int32)


def steps_of(own_key, extent, shards, smallest, top_value):
    gain = 1.0
    for dim, parts in shards:
        draws = jax.random.uniform(jax.random.fold_in(jax.random.fold_in(own_key, 6), dim), (parts,), jnp.float32, smallest / len(shards), top_value / len(shards))
        gain = gain * jnp.repeat(jnp.exp(draws), extent[dim] // parts).reshape((-1,) + (1,) * (len(extent) - 1 - dim))
    return gain


def scatter_about(own_key, extent, scale, most, shards=(), kind=jnp.bfloat16):
    entries = scale * jax.random.normal(own_key, extent, jnp.float32)
    if shards:
        entries = entries * steps_of(own_key, extent, shards, -0.22, 0.18)
    return jnp.clip(entries, -most, most).astype(kind)


def setup_inputs(seed: int = 0) -> dict:
    arg_keys = jax.random.split(jax.random.key(seed), 11)
    text_rows = scatter_about(arg_keys[0], (ITEMS, SEGS_MAX, TEXT, D), 1.0, 6.0, ((0, 32),))
    attn_weight = draw_attn_weight(jax.random.fold_in(arg_keys[10], 71), 0)
    vectors = draw_vectors(jax.random.fold_in(arg_keys[10], 71), 0)
    w_in = scatter_about(arg_keys[3], (D, FF), D ** -0.5, 0.21875, ((0, 8), (1, 4)))
    b_in = scatter_about(arg_keys[4], (N_FFN, FF // N_FFN), 0.3, 1.5, ((0, 4), (1, 8)))
    w_out = scatter_about(arg_keys[5], (FF, D), FF ** -0.5, 0.109375, ((0, 4), (1, 8)))
    seg_count = draw_seg_count(jax.random.fold_in(arg_keys[10], 71), 0)
    last_fill = draw_last_fill(jax.random.fold_in(arg_keys[10], 71), 0)
    out_grad = scatter_about(arg_keys[8], (ITEMS, SEGS_MAX, TEXT, D), 1.0, 6.0, ((0, 32),))
    mem_grad = scatter_about(arg_keys[9], (ITEMS, MEM, D), 1.0, 6.0, ((0, 32),), jnp.float32)
    return {"text_rows": text_rows, "attn_weight": attn_weight, "vectors": vectors, "w_in": w_in, "b_in": b_in, "w_out": w_out, "seg_count": seg_count, "last_fill": last_fill, "out_grad": out_grad, "mem_grad": mem_grad}


epsilon = 1e-12
root_half = 0.7071067811865476
highest = lax.Precision.HIGHEST

@jax.custom_vjp
def low(v):
    return lax.optimization_barrier(v.astype(jnp.bfloat16)).astype(jnp.float32)

@jax.custom_vjp
def low_back(v):
    return v

def low_keep(v):
    return (low(v), None)

def low_pass(kept, grad):
    return (grad,)

def back_keep(v):
    return (v, None)

def back_low(kept, grad):
    return (low(grad),)
low.defvjp(low_keep, low_pass)
low_back.defvjp(back_keep, back_low)

def round_both(value):
    return low_back(low(value))

def matmul_high(left, right):
    return jnp.dot(left, right, precision=highest, preferred_element_type=jnp.float32)

def gelu_value(pre_act):
    return 0.5 * pre_act * (1.0 + lax.erf(pre_act * root_half))

def layer_norm(value, gain_row, shift_row):
    centered = value - lax.optimization_barrier(jnp.mean(value, axis=-1, keepdims=True))
    inverse = lax.rsqrt(lax.optimization_barrier(jnp.mean(centered * centered, axis=-1, keepdims=True)) + epsilon)
    return centered * inverse * gain_row + shift_row

def segment_layer(joined, key_keep, attn_all, small_params, w_first, b_first, w_second):
    seg_rows, model_width = joined.shape
    joined_low = low(joined)
    queries = round_both(matmul_high(joined_low, attn_all[:model_width]) + small_params[0])
    key_rows = round_both(matmul_high(joined_low, attn_all[model_width:2 * model_width]))
    values = round_both(matmul_high(joined_low, attn_all[2 * model_width:3 * model_width]) + small_params[1])
    query_heads = queries.reshape(seg_rows, HEADS, HD)
    key_heads = key_rows.reshape(seg_rows, HEADS, HD)
    value_heads = values.reshape(seg_rows, HEADS, HD)
    raw_scores = jnp.einsum('qhd,khd->hqk', query_heads, key_heads, precision=highest) * HD ** (-0.5)
    scores = low_back(raw_scores) + ((key_keep - 1.0) * 1000000000.0)[None, None, :]
    row_peak = lax.optimization_barrier(jnp.max(scores, axis=-1, keepdims=True))
    exponent = jnp.exp(scores - row_peak)
    attn_probs = low(exponent / lax.optimization_barrier(jnp.sum(exponent, axis=-1, keepdims=True)))
    mixed = jnp.einsum('hqk,khd->qhd', attn_probs, value_heads, precision=highest)
    mixed = round_both(mixed.reshape(seg_rows, model_width))
    attn_out = low_back(matmul_high(mixed, attn_all[3 * model_width:]) + small_params[2])
    normed = layer_norm(joined + attn_out, small_params[3], small_params[4])
    hidden_pre = low_back(matmul_high(low(normed), w_first) + b_first)
    branch = low_back(matmul_high(low(gelu_value(hidden_pre)), w_second) + small_params[5])
    return layer_norm(normed + branch, small_params[6], small_params[7])

def item_forward(params, item_text, seg_total, fill_count):
    attn_all, small_params, w_first, b_first, w_second = params
    memory = small_params[8:8 + MEM]
    position = jnp.arange(TEXT)
    seg_outs = []
    for seg_index in range(SEGS_MAX):
        active = seg_index < seg_total
        fill_limit = jnp.where(seg_index == seg_total - 1, fill_count, jnp.where(active, TEXT, 0))
        keep_text = (position < fill_limit).astype(jnp.float32)
        mem_ones = jnp.ones((MEM,), jnp.float32)
        key_keep = jnp.concatenate([mem_ones, keep_text, mem_ones])
        joined = jnp.concatenate([memory, item_text[seg_index], memory], axis=0)
        result = segment_layer(joined, key_keep, attn_all, small_params, w_first, b_first, w_second)
        seg_outs.append(result[MEM:MEM + TEXT] * keep_text[:, None])
        memory = jnp.where(active, result[MEM + TEXT:], memory)
    return (jnp.stack(seg_outs), memory)

def reference(text_rows, attn_weight, vectors, w_in, b_in, w_out, seg_count, last_fill, out_grad, mem_grad):
    params = (attn_weight.astype(jnp.float32), vectors.astype(jnp.float32), w_in.astype(jnp.float32), b_in.reshape(-1).astype(jnp.float32), w_out.astype(jnp.float32))
    inputs = text_rows.astype(jnp.float32)

    def run_all(params, inputs):

        def one_item(packed):
            item_text, seg_total, fill_count = packed
            return jax.checkpoint(item_forward)(params, item_text, seg_total, fill_count)
        return lax.map(one_item, (inputs, seg_count, last_fill))
    (seg_outs, memory), pullback = jax.vjp(run_all, params, inputs)
    param_grads, input_grad = pullback((out_grad.astype(jnp.float32), mem_grad.astype(jnp.float32)))
    attn_grad, vector_grad, first_grad, bias_grad, second_grad = param_grads
    return (seg_outs.astype(jnp.bfloat16), memory, input_grad, attn_grad, vector_grad, first_grad, bias_grad.reshape(N_FFN, FF // N_FFN), second_grad)
```

```python
import functools

import jax
import jax.numpy as jnp
from jax import lax
from jax.experimental import pallas as pl
from jax.experimental.pallas import tpu as pltpu
from jax.sharding import PartitionSpec as P

HEADS = 12
HD = 64
MEM = 10
TEXT = 502
SEGS_MAX = 4
ROWS = TEXT + MEM
AUG = 16

epsilon = 1e-12
root_half = 0.7071067811865476
inv_root_tau = 0.3989422804014327
log_two = 0.6931471805599453

f32 = jnp.float32
bf16 = jnp.bfloat16
AXES = ("items", "ffn")


def dot_nn(a, b):
    return jnp.dot(a, b, preferred_element_type=f32)


def dot_nt(a, b):
    return lax.dot_general(a, b, (((1,), (1,)), ((), ())), preferred_element_type=f32)


def dot_tn(a, b):
    return lax.dot_general(a, b, (((0,), (0,)), ((), ())), preferred_element_type=f32)


def split_three(value):
    high = value.astype(bf16)
    rest = value - high.astype(f32)
    mid = rest.astype(bf16)
    last = (rest - mid.astype(f32)).astype(bf16)
    return high, mid, last


def gelu_both(pre):
    half = 0.5 * (1.0 + lax.erf(pre * root_half))
    slope = half + pre * jnp.exp(-0.5 * pre * pre) * inv_root_tau
    return pre * half, slope


def norm_rows(value):
    centered = value - jnp.mean(value, axis=-1, keepdims=True)
    inverse = lax.rsqrt(jnp.mean(centered * centered, axis=-1, keepdims=True) + epsilon)
    return centered * inverse, inverse


def norm_rows_back(upstream, normed, inverse, gain):
    scaled = upstream * gain
    return inverse * (
        scaled
        - jnp.mean(scaled, axis=-1, keepdims=True)
        - normed * jnp.mean(scaled * normed, axis=-1, keepdims=True)
    )


def fill_limit(seg, count, fill):
    return jnp.where(seg < count, jnp.where(seg == count - 1, fill, TEXT), 0)


def aug_rows(first, second):
    width = first[0].shape[1]
    row = lax.broadcasted_iota(jnp.int32, (AUG, width), 0)
    out = jnp.zeros((AUG, width), f32)
    for place, piece in enumerate(tuple(first) + tuple(second)):
        out = jnp.where(row == place, jnp.broadcast_to(piece.astype(f32), (AUG, width)), out)
    return out.astype(bf16)


def ones_three(width):
    one = jnp.ones((1, width), bf16)
    return (one, one, one)


def key_bias(limit):
    place = lax.broadcasted_iota(jnp.int32, (1, ROWS), 1)
    bias = jnp.where(place < limit, 0.0, jnp.where(place < TEXT, -1e9, log_two)).astype(f32)
    return split_three(bias)


def forward_kernel(
    count_ref, fill_ref, text_ref, attn_ref, win_ref, wout_ref, bin_ref, vec_ref, col_ref,
    out_ref, mem_ref, zl_ref, qkv_ref, mixed_ref, lse_ref, n1_ref, r1_ref, hl_ref, act_ref,
    slope_ref, n2_ref, r2_ref,
    memory, z_ref, h_ref, acc_ref,
):
    seg = pl.program_id(0)
    count, fill = count_ref[0], fill_ref[0]
    limit = fill_limit(seg, count, fill)
    width = z_ref.shape[1]

    @pl.when(seg == 0)
    def _():
        memory[...] = vec_ref[8 : 8 + MEM, :]

    z_ref[:TEXT, :] = text_ref[0].astype(f32)
    z_ref[TEXT:, :] = memory[...]
    zl = z_ref[...].astype(bf16)
    zl_ref[...] = zl
    for c in range(3):
        part = dot_nt(attn_ref[c * width : (c + 1) * width, :], zl)
        if c == 0:
            part = (part + col_ref[:, 0:1]).astype(bf16) * jnp.asarray(HD ** (-0.5), bf16)
        elif c == 2:
            part = (part + col_ref[:, 1:2]).astype(bf16)
        else:
            part = part.astype(bf16)
        qkv_ref[c * width : (c + 1) * width, :] = part

    ones = ones_three(ROWS)
    key_aug = aug_rows(key_bias(limit), ())
    query_aug = aug_rows(ones, ())
    for head in range(HEADS):
        lo = head * HD
        q_aug = jnp.concatenate([qkv_ref[lo : lo + HD, :], query_aug], axis=0)
        k_aug = jnp.concatenate([qkv_ref[width + lo : width + lo + HD, :], key_aug], axis=0)
        v_aug = jnp.concatenate([qkv_ref[2 * width + lo : 2 * width + lo + HD, :], query_aug], axis=0)
        scores = dot_tn(k_aug, q_aug)
        peak = jnp.max(scores, axis=0, keepdims=True)
        expo = jnp.exp(scores - peak).astype(bf16)
        both = dot_nn(v_aug, expo)
        total = both[HD : HD + 1, :]
        mixed_ref[lo : lo + HD, :] = (both[:HD, :] * (1.0 / total)).astype(bf16)
        lse_ref[0, head : head + 1, :] = peak + jnp.log(total)

    first = z_ref[...] + (dot_tn(mixed_ref[...], attn_ref[3 * width :, :]) + vec_ref[2:3, :])
    normed, inverse = norm_rows(first)
    n1_ref[...] = normed.astype(bf16)
    r1_ref[...] = inverse
    h = normed * vec_ref[3:4, :] + vec_ref[4:5, :]
    h_ref[...] = h
    hl_ref[...] = h.astype(bf16)

    blocks, _, block = win_ref.shape
    for f in range(blocks):
        pre = dot_nn(hl_ref[...], win_ref[f]) + bin_ref[f : f + 1, :]
        act, slope = gelu_both(pre)
        act_ref[:, f * block : (f + 1) * block] = act.astype(bf16)
        slope_ref[:, f * block : (f + 1) * block] = slope.astype(bf16)
        part = dot_nt(act_ref[:, f * block : (f + 1) * block], wout_ref[f])
        if f == 0:
            acc_ref[...] = part
        else:
            acc_ref[...] += part

    normed, inverse = norm_rows(h_ref[...] + (acc_ref[...] + vec_ref[5:6, :]))
    n2_ref[...] = normed.astype(bf16)
    r2_ref[...] = inverse
    y = normed * vec_ref[6:7, :] + vec_ref[7:8, :]
    row = lax.broadcasted_iota(jnp.int32, (TEXT, 1), 0)
    out_ref[0] = jnp.where(row < limit, y[:TEXT, :], 0.0).astype(bf16)
    memory[...] = jnp.where(seg < count, y[TEXT:, :], memory[...])
    mem_ref[...] = memory[...]


def backward_kernel(
    count_ref, fill_ref, grad_ref, mgrad_ref, attn_ref, win_ref, wout_ref, vec_ref,
    qkv_ref, mixed_ref, lse_ref, n1_ref, r1_ref, slope_ref, n2_ref, r2_ref,
    tgrad_ref, gbranch_ref, gpre_ref, gattn_ref, gqkv_ref, vgrad_ref, bgrad_ref, gmem_ref,
    gm_ref, gy_ref, second_ref, acc_ref, mix_ref, cols_ref,
):
    step = pl.program_id(0)
    seg = SEGS_MAX - 1 - step
    count, fill = count_ref[0], fill_ref[0]
    limit = fill_limit(seg, count, fill)
    width = gy_ref.shape[1]

    @pl.when(step == 0)
    def _():
        gm_ref[...] = mgrad_ref[0]
        vgrad_ref[...] = jnp.zeros_like(vgrad_ref)
        bgrad_ref[...] = jnp.zeros_like(bgrad_ref)

    row = lax.broadcasted_iota(jnp.int32, (TEXT, 1), 0)
    gy_ref[:TEXT, :] = jnp.where(row < limit, grad_ref[0].astype(f32), 0.0)
    gy_ref[TEXT:, :] = jnp.where(seg < count, gm_ref[...], 0.0)

    def column_sum(value):
        return jnp.sum(value, axis=0, keepdims=True)

    gy = gy_ref[...]
    normed = n2_ref[...].astype(f32)
    vgrad_ref[6:7, :] += column_sum(gy * normed)
    vgrad_ref[7:8, :] += column_sum(gy)
    second = norm_rows_back(gy, normed, r2_ref[...], vec_ref[6:7, :])
    second_ref[...] = second
    gbranch_ref[...] = second.astype(bf16)
    vgrad_ref[5:6, :] += column_sum(gbranch_ref[...].astype(f32))

    blocks, _, block = win_ref.shape
    for f in range(blocks):
        sl = slice(f * block, (f + 1) * block)
        hidden = dot_nn(gbranch_ref[...], wout_ref[f])
        pre = (hidden * slope_ref[:, sl].astype(f32)).astype(bf16)
        gpre_ref[:, sl] = pre
        bgrad_ref[f : f + 1, :] += column_sum(pre.astype(f32))
        part = dot_nt(gpre_ref[:, sl], win_ref[f])
        if f == 0:
            acc_ref[...] = part
        else:
            acc_ref[...] += part

    gh = second_ref[...] + acc_ref[...]
    normed = n1_ref[...].astype(f32)
    vgrad_ref[3:4, :] += column_sum(gh * normed)
    vgrad_ref[4:5, :] += column_sum(gh)
    first = norm_rows_back(gh, normed, r1_ref[...], vec_ref[3:4, :])
    second_ref[...] = first
    gattn_ref[...] = first.astype(bf16)
    vgrad_ref[2:3, :] += column_sum(gattn_ref[...].astype(f32))
    mix_ref[...] = dot_nt(attn_ref[3 * width :, :], gattn_ref[...]).astype(bf16)

    ones = ones_three(ROWS)
    key_aug = aug_rows(key_bias(limit), ones)
    value_aug = aug_rows(ones, ())
    for head in range(HEADS):
        lo = head * HD
        q_h = qkv_ref[lo : lo + HD, :]
        k_h = qkv_ref[width + lo : width + lo + HD, :]
        v_h = qkv_ref[2 * width + lo : 2 * width + lo + HD, :]
        g_h = mix_ref[lo : lo + HD, :]
        inner = column_sum(g_h.astype(f32) * mixed_ref[lo : lo + HD, :].astype(f32))
        q_aug = jnp.concatenate([q_h, aug_rows(ones, split_three(-lse_ref[0, head : head + 1, :]))], axis=0)
        k_aug = jnp.concatenate([k_h, key_aug], axis=0)
        v_aug = jnp.concatenate([v_h, value_aug], axis=0)
        g_aug = jnp.concatenate([g_h, aug_rows(split_three(-inner), ())], axis=0)
        probs = jnp.exp(dot_tn(k_aug, q_aug))
        grads = (probs * dot_tn(v_aug, g_aug)).astype(bf16)
        probs_low = probs.astype(bf16)
        cols_ref[lo : lo + HD, :] = dot_nn(k_h, grads) * (HD ** (-0.5))
        cols_ref[width + lo : width + lo + HD, :] = dot_nt(q_h, grads)
        cols_ref[2 * width + lo : 2 * width + lo + HD, :] = dot_nt(g_h, probs_low)

    for c in range(3):
        gqkv_ref[:, c * width : (c + 1) * width] = cols_ref[c * width : (c + 1) * width, :].T.astype(bf16)
    vgrad_ref[0:1, :] += column_sum(gqkv_ref[:, :width].astype(f32))
    vgrad_ref[1:2, :] += column_sum(gqkv_ref[:, 2 * width :].astype(f32))
    joined = second_ref[...]
    for c in range(3):
        joined = joined + dot_nt(gqkv_ref[:, c * width : (c + 1) * width], attn_ref[c * width : (c + 1) * width, :])
    acc_ref[...] = joined
    tgrad_ref[0] = acc_ref[:TEXT, :]
    gm_ref[...] = jnp.where(seg < count, acc_ref[TEXT:, :], gm_ref[...])
    gmem_ref[...] = gm_ref[...]


def whole():
    return pl.BlockSpec(memory_space=pltpu.VMEM)


def scalar():
    return pl.BlockSpec(memory_space=pltpu.SMEM)


def forward_call(count, fill, text, attn_t, win, wout, bias, vec, col):
    width = text.shape[-1]
    hidden = win.shape[0] * win.shape[2]
    total = SEGS_MAX * ROWS

    def rows(cols):
        return pl.BlockSpec((ROWS, cols), lambda s: (s, 0))

    def lanes(height):
        return pl.BlockSpec((height, ROWS), lambda s: (0, s))

    seg_block = pl.BlockSpec((1, TEXT, width), lambda s: (s, 0, 0))
    sds = jax.ShapeDtypeStruct
    return pl.pallas_call(
        forward_kernel,
        grid=(SEGS_MAX,),
        in_specs=[scalar(), scalar(), seg_block] + [whole()] * 6,
        out_specs=[
            seg_block, pl.BlockSpec((MEM, width), lambda s: (0, 0)),
            rows(width), lanes(3 * width), lanes(width),
            pl.BlockSpec((1, 16, ROWS), lambda s: (s, 0, 0)),
            rows(width), rows(1), rows(width), rows(hidden), rows(hidden), rows(width), rows(1),
        ],
        out_shape=[
            sds((SEGS_MAX, TEXT, width), bf16), sds((MEM, width), f32),
            sds((total, width), bf16), sds((3 * width, total), bf16), sds((width, total), bf16),
            sds((SEGS_MAX, 16, ROWS), f32),
            sds((total, width), bf16), sds((total, 1), f32), sds((total, width), bf16),
            sds((total, hidden), bf16), sds((total, hidden), bf16), sds((total, width), bf16),
            sds((total, 1), f32),
        ],
        scratch_shapes=[
            pltpu.VMEM((MEM, width), f32), pltpu.VMEM((ROWS, width), f32),
            pltpu.VMEM((ROWS, width), f32), pltpu.VMEM((ROWS, width), f32),
        ],
        compiler_params=pltpu.CompilerParams(vmem_limit_bytes=62 * 2**20),
    )(count, fill, text, attn_t, win, wout, bias, vec, col)


def backward_call(count, fill, out_grad, mem_grad, attn, win, wout, vec, saved):
    width = out_grad.shape[-1]
    blocks, _, block = win.shape
    hidden = blocks * block
    total = SEGS_MAX * ROWS
    last = SEGS_MAX - 1

    def rows(cols):
        return pl.BlockSpec((ROWS, cols), lambda s: (last - s, 0))

    def lanes(height):
        return pl.BlockSpec((height, ROWS), lambda s: (0, last - s))

    def fixed(*shape):
        return pl.BlockSpec(shape, lambda s: (0,) * len(shape))

    seg_block = pl.BlockSpec((1, TEXT, width), lambda s: (last - s, 0, 0))
    sds = jax.ShapeDtypeStruct
    return pl.pallas_call(
        backward_kernel,
        grid=(SEGS_MAX,),
        in_specs=[scalar(), scalar(), seg_block] + [whole()] * 5
        + [
            lanes(3 * width), lanes(width), pl.BlockSpec((1, 16, ROWS), lambda s: (last - s, 0, 0)),
            rows(width), rows(1), rows(hidden), rows(width), rows(1),
        ],
        out_specs=[
            seg_block, rows(width), rows(hidden), rows(width), rows(3 * width),
            fixed(8, width), fixed(blocks, block), fixed(MEM, width),
        ],
        out_shape=[
            sds((SEGS_MAX, TEXT, width), f32), sds((total, width), bf16), sds((total, hidden), bf16),
            sds((total, width), bf16), sds((total, 3 * width), bf16),
            sds((8, width), f32), sds((blocks, block), f32), sds((MEM, width), f32),
        ],
        scratch_shapes=[
            pltpu.VMEM((MEM, width), f32), pltpu.VMEM((ROWS, width), f32),
            pltpu.VMEM((ROWS, width), f32), pltpu.VMEM((ROWS, width), f32),
            pltpu.VMEM((width, ROWS), bf16), pltpu.VMEM((3 * width, ROWS), f32),
        ],
        compiler_params=pltpu.CompilerParams(vmem_limit_bytes=62 * 2**20),
    )(count, fill, out_grad, mem_grad, attn, win, wout, vec, *saved)


def body(n_items, n_ffn, text_rows, attn_weight, vectors, w_in, b_in, w_out, seg_count, last_fill, out_grad, mem_grad):
    width = text_rows.shape[-1]
    block = w_in.shape[1]
    attn = lax.all_gather(attn_weight, AXES, axis=0, tiled=True)
    vec = lax.all_gather(vectors, AXES, axis=1, tiled=True).astype(f32)

    def by_block(shard):
        parts = lax.all_gather(shard, AXES, axis=0).reshape(n_items, n_ffn, width // n_items, block)
        return parts.transpose(1, 0, 2, 3).reshape(n_ffn, width, block)

    win = by_block(w_in)
    wout = by_block(w_out.T)
    bias = lax.all_gather(b_in, AXES, axis=0).reshape(n_items, n_ffn, -1)
    bias = bias.transpose(1, 0, 2).reshape(n_ffn, block).astype(f32)
    attn_t = jnp.concatenate(
        [attn[: 3 * width].reshape(3, width, width).transpose(0, 2, 1).reshape(3 * width, width), attn[3 * width :]]
    )
    col = vec[:2].T

    (activations, memory, zl, qkv, mixed, lse, n1, r1, hl, act, slope, n2, r2) = forward_call(
        seg_count, last_fill, text_rows[0], attn_t, win, wout, bias, vec, col
    )
    text_grad, gbranch, gpre, gattn, gqkv, vgrad, bgrad, gmem = backward_call(
        seg_count, last_fill, out_grad[0], mem_grad, attn, win, wout, vec,
        (qkv, mixed, lse, n1, r1, slope, n2, r2),
    )

    def scatter_block(grad):
        grad = grad.astype(bf16).reshape(n_items, width // n_items, n_ffn, block).transpose(0, 2, 1, 3)
        return lax.psum_scatter(grad.reshape(n_items * n_ffn, width // n_items, block), AXES, scatter_dimension=0, tiled=False).astype(f32)

    w_out_grad = scatter_block(dot_tn(gbranch, act)).T
    w_in_grad = scatter_block(dot_tn(hl, gpre))
    three = dot_tn(zl, gqkv)
    attn_total = jnp.concatenate(
        [three[:, c * width : (c + 1) * width] for c in range(3)] + [dot_nn(mixed, gattn)], axis=0
    ).astype(bf16)
    attn_grad = lax.psum_scatter(attn_total, AXES, scatter_dimension=0, tiled=True).astype(f32)
    vec_total = jnp.concatenate([vgrad, gmem], axis=0)
    vector_grad = lax.psum_scatter(vec_total, AXES, scatter_dimension=1, tiled=True)
    b_total = bgrad.reshape(n_ffn, n_items, block // n_items).transpose(1, 0, 2).reshape(n_items * n_ffn, 1, block // n_items)
    b_in_grad = lax.psum_scatter(b_total, AXES, scatter_dimension=0, tiled=False)
    return (activations[None], memory[None], text_grad[None], attn_grad, vector_grad, w_in_grad, b_in_grad, w_out_grad)


def solution(mesh):
    both = P(AXES)
    return jax.shard_map(
        functools.partial(body, mesh.shape["items"], mesh.shape["ffn"]),
        mesh=mesh,
        in_specs=(
            both, both, P(None, AXES), P("items", "ffn"), P("ffn", "items"), P("ffn", "items"),
            both, both, both, both,
        ),
        out_specs=(both, both, both, both, P(None, AXES), P("items", "ffn"), P("ffn", "items"), P("ffn", "items")),
        check_vma=False,
    )
```

```python
import functools

import jax
import jax.numpy as jnp
from jax import lax
from jax.experimental import pallas as pl
from jax.experimental.layout import Layout, with_layout_constraint
from jax.experimental.pallas import tpu as pltpu
from jax.sharding import PartitionSpec as P

HEADS = 12
HD = 64
MEM = 10
TEXT = 502
SEGS_MAX = 4
ROWS = TEXT + MEM
AUG = 16

epsilon = 1e-12
root_half = 0.7071067811865476
inv_root_tau = 0.3989422804014327
log_two = 0.6931471805599453

f32 = jnp.float32
bf16 = jnp.bfloat16
AXES = ("items", "ffn")


def dot_nn(a, b):
    return jnp.dot(a, b, preferred_element_type=f32)


def dot_nt(a, b):
    return lax.dot_general(a, b, (((1,), (1,)), ((), ())), preferred_element_type=f32)


def dot_tn(a, b):
    return lax.dot_general(a, b, (((0,), (0,)), ((), ())), preferred_element_type=f32)


def split_three(value):
    high = value.astype(bf16)
    rest = value - high.astype(f32)
    mid = rest.astype(bf16)
    last = (rest - mid.astype(f32)).astype(bf16)
    return high, mid, last


def gelu_both(pre):
    half = 0.5 * (1.0 + lax.erf(pre * root_half))
    slope = half + pre * jnp.exp(-0.5 * pre * pre) * inv_root_tau
    return pre * half, slope


def norm_rows(value):
    centered = value - jnp.mean(value, axis=-1, keepdims=True)
    inverse = lax.rsqrt(jnp.mean(centered * centered, axis=-1, keepdims=True) + epsilon)
    return centered * inverse, inverse


def norm_rows_back(upstream, normed, inverse, gain):
    scaled = upstream * gain
    return inverse * (
        scaled
        - jnp.mean(scaled, axis=-1, keepdims=True)
        - normed * jnp.mean(scaled * normed, axis=-1, keepdims=True)
    )


def fill_limit(seg, count, fill):
    return jnp.where(seg < count, jnp.where(seg == count - 1, fill, TEXT), 0)


def aug_rows(first, second):
    width = first[0].shape[1]
    row = lax.broadcasted_iota(jnp.int32, (AUG, width), 0)
    out = jnp.zeros((AUG, width), f32)
    for place, piece in enumerate(tuple(first) + tuple(second)):
        out = jnp.where(row == place, jnp.broadcast_to(piece.astype(f32), (AUG, width)), out)
    return out.astype(bf16)


def ones_three(width):
    one = jnp.ones((1, width), bf16)
    return (one, one, one)


def key_bias(limit):
    place = lax.broadcasted_iota(jnp.int32, (1, ROWS), 1)
    bias = jnp.where(place < limit, 0.0, jnp.where(place < TEXT, -1e9, log_two)).astype(f32)
    return split_three(bias)


def start_loads(table_ref, pieces, plan, targets, sems, wanted):
    for place, (piece, start, rows, target) in enumerate(plan):
        if target not in wanted:
            continue
        dest = pl.multiple_of(table_ref[place], rows)
        pltpu.make_async_copy(
            pieces[piece].at[pl.ds(start, rows), :], targets[target].at[pl.ds(dest, rows), :], sems.at[target]
        ).start()


def wait_loads(targets, sems, target):
    pltpu.make_async_copy(targets[target], targets[target], sems.at[target]).wait()


def forward_kernel(
    plan, n_pieces, count_ref, fill_ref, table_ref, text_ref, bin_ref, vec_ref, col_ref, *refs,
):
    pieces, refs = refs[:n_pieces], refs[n_pieces:]
    forward_segment(plan, pieces, count_ref, fill_ref, table_ref, text_ref, bin_ref, vec_ref, col_ref, *refs)


def forward_segment(
    plan, pieces, count_ref, fill_ref, table_ref, text_ref, bin_ref, vec_ref, col_ref,
    out_ref, mem_ref, zl_ref, qkv_ref, mixed_ref, lse_ref, n1_ref, r1_ref, hl_ref, act_ref,
    slope_ref, n2_ref, r2_ref,
    memory, z_ref, h_ref, acc_ref, attn_ref, win_ref, wout_ref, turned_ref, sems,
):
    weights = (attn_ref, win_ref, wout_ref)
    seg = pl.program_id(0)
    count, fill = count_ref[0], fill_ref[0]
    limit = fill_limit(seg, count, fill)
    width = z_ref.shape[1]

    @pl.when(seg == 0)
    def _():
        start_loads(table_ref, pieces, plan, weights, sems, (0,))
        memory[...] = vec_ref[8 : 8 + MEM, :]
        wait_loads(weights, sems, 0)
        start_loads(table_ref, pieces, plan, weights, sems, (1, 2))
        for c in range(3):
            turned_ref[c * width : (c + 1) * width, :] = attn_ref[c * width : (c + 1) * width, :].T

    z_ref[:TEXT, :] = text_ref[0].astype(f32)
    z_ref[TEXT:, :] = memory[...]
    zl = z_ref[...].astype(bf16)
    zl_ref[...] = zl
    for c in range(3):
        part = dot_nt(turned_ref[c * width : (c + 1) * width, :], zl)
        if c == 0:
            part = (part + col_ref[:, 0:1]).astype(bf16) * jnp.asarray(HD ** (-0.5), bf16)
        elif c == 2:
            part = (part + col_ref[:, 1:2]).astype(bf16)
        else:
            part = part.astype(bf16)
        qkv_ref[c * width : (c + 1) * width, :] = part

    ones = ones_three(ROWS)
    key_aug = aug_rows(key_bias(limit), ())
    query_aug = aug_rows(ones, ())

    def scores_of(head):
        lo = head * HD
        q_aug = jnp.concatenate([qkv_ref[lo : lo + HD, :], query_aug], axis=0)
        k_aug = jnp.concatenate([qkv_ref[width + lo : width + lo + HD, :], key_aug], axis=0)
        return dot_tn(k_aug, q_aug)

    def mix(head, peak, expo):
        lo = head * HD
        v_aug = jnp.concatenate([qkv_ref[2 * width + lo : 2 * width + lo + HD, :], query_aug], axis=0)
        both = dot_nn(v_aug, expo)
        total = both[HD : HD + 1, :]
        mixed_ref[lo : lo + HD, :] = (both[:HD, :] * (1.0 / total)).astype(bf16)
        lse_ref[0, head : head + 1, :] = peak + jnp.log(total)

    scores, held = scores_of(0), None
    for head in range(HEADS):
        following = scores_of(head + 1) if head + 1 < HEADS else None
        if held is not None:
            mix(head - 1, *held)
        peak = jnp.max(scores, axis=0, keepdims=True)
        held = peak, jnp.exp(scores - peak).astype(bf16)
        scores = following
    mix(HEADS - 1, *held)

    first = z_ref[...] + (dot_tn(mixed_ref[...], attn_ref[3 * width :, :]) + vec_ref[2:3, :])
    normed, inverse = norm_rows(first)
    n1_ref[...] = normed.astype(bf16)
    r1_ref[...] = inverse
    h = normed * vec_ref[3:4, :] + vec_ref[4:5, :]
    h_ref[...] = h
    hl_ref[...] = h.astype(bf16)

    @pl.when(seg == 0)
    def _():
        wait_loads(weights, sems, 1)
        wait_loads(weights, sems, 2)

    blocks, block = bin_ref.shape
    for low in range(0, ROWS, ROWS // 2):
        rs = slice(low, low + ROWS // 2)
        for f in range(blocks):
            sl, cs = slice(f * width, (f + 1) * width), slice(f * block, (f + 1) * block)
            pre = dot_nn(hl_ref[rs, :], win_ref[sl, :]) + bin_ref[f : f + 1, :]
            act, slope = gelu_both(pre)
            act_ref[rs, cs] = act.astype(bf16)
            slope_ref[rs, cs] = slope.astype(bf16)
        part = dot_nt(act_ref[rs, :block], wout_ref[:width, :])
        for f in range(1, blocks):
            part += dot_nt(act_ref[rs, f * block : (f + 1) * block], wout_ref[f * width : (f + 1) * width, :])
        acc_ref[rs, :] = part

    normed, inverse = norm_rows(h_ref[...] + (acc_ref[...] + vec_ref[5:6, :]))
    n2_ref[...] = normed.astype(bf16)
    r2_ref[...] = inverse
    y = normed * vec_ref[6:7, :] + vec_ref[7:8, :]
    row = lax.broadcasted_iota(jnp.int32, (TEXT, 1), 0)
    out_ref[0] = jnp.where(row < limit, y[:TEXT, :], 0.0).astype(bf16)
    memory[...] = jnp.where(seg < count, y[TEXT:, :], memory[...])
    mem_ref[...] = memory[...]


def backward_kernel(
    plan, n_pieces, count_ref, fill_ref, table_ref, grad_ref, mgrad_ref, vec_ref, *refs,
):
    pieces, refs = refs[:n_pieces], refs[n_pieces:]
    backward_segment(plan, pieces, count_ref, fill_ref, table_ref, grad_ref, mgrad_ref, vec_ref, *refs)


def backward_segment(
    plan, pieces, count_ref, fill_ref, table_ref, grad_ref, mgrad_ref, vec_ref,
    qkv_ref, mixed_ref, lse_ref, n1_ref, r1_ref, slope_ref, n2_ref, r2_ref,
    first_ref, gbranch_ref, gpre_ref, gattn_ref, gqkv_ref, vgrad_ref, bgrad_ref, gmem_ref,
    edge_ref, gm_ref, gy_ref, second_ref, acc_ref, mix_ref, cols_ref, attn_ref, win_ref, wout_ref, sems,
):
    weights = (attn_ref, win_ref, wout_ref)
    step = pl.program_id(0)
    seg = SEGS_MAX - 1 - step
    count, fill = count_ref[0], fill_ref[0]
    limit = fill_limit(seg, count, fill)
    width = gy_ref.shape[1]

    @pl.when(step == 0)
    def _():
        start_loads(table_ref, pieces, plan, weights, sems, (1, 2))
        gm_ref[...] = mgrad_ref[0]
        vgrad_ref[...] = jnp.zeros_like(vgrad_ref)
        bgrad_ref[...] = jnp.zeros_like(bgrad_ref)

    row = lax.broadcasted_iota(jnp.int32, (TEXT, 1), 0)
    gy_ref[:TEXT, :] = jnp.where(row < limit, grad_ref[0].astype(f32), 0.0)
    gy_ref[TEXT:, :] = jnp.where(seg < count, gm_ref[...], 0.0)

    def column_sum(value):
        return jnp.sum(value, axis=0, keepdims=True)

    gy = gy_ref[...]
    normed = n2_ref[...].astype(f32)
    vgrad_ref[6:7, :] += column_sum(gy * normed)
    vgrad_ref[7:8, :] += column_sum(gy)
    second = norm_rows_back(gy, normed, r2_ref[...], vec_ref[6:7, :])
    second_ref[...] = second
    gbranch_ref[...] = second.astype(bf16)
    vgrad_ref[5:6, :] += column_sum(gbranch_ref[...].astype(f32))

    @pl.when(step == 0)
    def _():
        wait_loads(weights, sems, 2)
        wait_loads(weights, sems, 1)
        start_loads(table_ref, pieces, plan, weights, sems, (0,))

    blocks, block = bgrad_ref.shape
    for f in range(blocks):
        sl = slice(f * block, (f + 1) * block)
        rows = slice(f * width, (f + 1) * width)
        hidden = dot_nn(gbranch_ref[...], wout_ref[rows, :])
        pre = (hidden * slope_ref[:, sl].astype(f32)).astype(bf16)
        gpre_ref[:, sl] = pre
        bgrad_ref[f : f + 1, :] += column_sum(pre.astype(f32))
        part = dot_nt(gpre_ref[:, sl], win_ref[rows, :])
        if f == 0:
            acc_ref[...] = part
        else:
            acc_ref[...] += part

    gh = second_ref[...] + acc_ref[...]
    normed = n1_ref[...].astype(f32)
    vgrad_ref[3:4, :] += column_sum(gh * normed)
    vgrad_ref[4:5, :] += column_sum(gh)
    first = norm_rows_back(gh, normed, r1_ref[...], vec_ref[3:4, :])
    second_ref[...] = first
    gattn_ref[...] = first.astype(bf16)
    vgrad_ref[2:3, :] += column_sum(gattn_ref[...].astype(f32))

    @pl.when(step == 0)
    def _():
        wait_loads(weights, sems, 0)

    mix_ref[...] = dot_nt(attn_ref[3 * width :, :], gattn_ref[...]).astype(bf16)

    ones = ones_three(ROWS)
    key_aug = aug_rows(key_bias(limit), ones)
    value_aug = aug_rows(ones, ())

    def maps_of(head):
        lo = head * HD
        q_h = qkv_ref[lo : lo + HD, :]
        k_h = qkv_ref[width + lo : width + lo + HD, :]
        v_h = qkv_ref[2 * width + lo : 2 * width + lo + HD, :]
        g_h = mix_ref[lo : lo + HD, :]
        inner = column_sum(g_h.astype(f32) * mixed_ref[lo : lo + HD, :].astype(f32))
        q_aug = jnp.concatenate([q_h, aug_rows(ones, split_three(-lse_ref[0, head : head + 1, :]))], axis=0)
        k_aug = jnp.concatenate([k_h, key_aug], axis=0)
        v_aug = jnp.concatenate([v_h, value_aug], axis=0)
        g_aug = jnp.concatenate([g_h, aug_rows(split_three(-inner), ())], axis=0)
        return dot_tn(q_aug, k_aug), dot_tn(g_aug, v_aug)

    def spread(head, grads, probs):
        lo = head * HD
        cols_ref[lo : lo + HD, :] = dot_nt(qkv_ref[width + lo : width + lo + HD, :], grads) * (HD ** (-0.5))
        cols_ref[width + lo : width + lo + HD, :] = dot_nn(qkv_ref[lo : lo + HD, :], grads)
        cols_ref[2 * width + lo : 2 * width + lo + HD, :] = dot_nn(mix_ref[lo : lo + HD, :], probs)

    maps = maps_of(0)
    for head in range(HEADS):
        following = maps_of(head + 1) if head + 1 < HEADS else None
        probs = jnp.exp(maps[0])
        spread(head, (probs * maps[1]).astype(bf16), probs.astype(bf16))
        maps = following

    for c in range(3):
        gqkv_ref[:, c * width : (c + 1) * width] = cols_ref[c * width : (c + 1) * width, :].T.astype(bf16)
    vgrad_ref[0:1, :] += column_sum(gqkv_ref[:, :width].astype(f32))
    vgrad_ref[1:2, :] += column_sum(gqkv_ref[:, 2 * width :].astype(f32))
    first_ref[...] = second_ref[...]
    edge = ROWS - AUG
    joined = second_ref[edge:, :]
    for c in range(3):
        joined = joined + dot_nt(gqkv_ref[edge:, c * width : (c + 1) * width], attn_ref[c * width : (c + 1) * width, :])
    edge_ref[...] = joined
    gm_ref[...] = jnp.where(seg < count, edge_ref[AUG - MEM :, :], gm_ref[...])
    gmem_ref[...] = gm_ref[...]


def whole():
    return pl.BlockSpec(memory_space=pltpu.VMEM)


def scalar():
    return pl.BlockSpec(memory_space=pltpu.SMEM)


def remain():
    return pl.BlockSpec(memory_space=pl.ANY)


def weight_scratch(width, blocks, block):
    return [
        pltpu.VMEM((4 * width, width), bf16), pltpu.VMEM((blocks * width, block), bf16),
        pltpu.VMEM((blocks * width, block), bf16),
    ]


def forward_call(count, fill, text, bias, vec, col, table, plan, pieces):
    width = text.shape[-1]
    blocks, block = bias.shape
    hidden = blocks * block
    total = SEGS_MAX * ROWS

    def rows(cols):
        return pl.BlockSpec((ROWS, cols), lambda s: (s, 0))

    def lanes(height):
        return pl.BlockSpec((height, ROWS), lambda s: (0, s))

    seg_block = pl.BlockSpec((1, TEXT, width), lambda s: (s, 0, 0))
    sds = jax.ShapeDtypeStruct
    return pl.pallas_call(
        functools.partial(forward_kernel, plan, len(pieces)),
        grid=(SEGS_MAX,),
        in_specs=[scalar(), scalar(), scalar(), seg_block] + [whole()] * 3 + [remain()] * len(pieces),
        out_specs=[
            seg_block, pl.BlockSpec((MEM, width), lambda s: (0, 0)),
            rows(width), lanes(3 * width), lanes(width),
            pl.BlockSpec((1, 16, ROWS), lambda s: (s, 0, 0)),
            rows(width), rows(1), rows(width), rows(hidden), rows(hidden), rows(width), rows(1),
        ],
        out_shape=[
            sds((SEGS_MAX, TEXT, width), bf16), sds((MEM, width), f32),
            sds((total, width), bf16), sds((3 * width, total), bf16), sds((width, total), bf16),
            sds((SEGS_MAX, 16, ROWS), f32),
            sds((total, width), bf16), sds((total, 1), f32), sds((total, width), bf16),
            sds((total, hidden), bf16), sds((total, hidden), bf16), sds((total, width), bf16),
            sds((total, 1), f32),
        ],
        scratch_shapes=[
            pltpu.VMEM((MEM, width), f32), pltpu.VMEM((ROWS, width), f32),
            pltpu.VMEM((ROWS, width), f32), pltpu.VMEM((ROWS, width), f32),
        ]
        + weight_scratch(width, blocks, block)
        + [pltpu.VMEM((3 * width, width), bf16), pltpu.SemaphoreType.DMA((3,))],
        compiler_params=pltpu.CompilerParams(vmem_limit_bytes=62 * 2**20),
    )(count, fill, table, text, bias, vec, col, *pieces)


def backward_call(count, fill, out_grad, mem_grad, vec, saved, shape, table, plan, pieces):
    width = out_grad.shape[-1]
    blocks, block = shape
    hidden = blocks * block
    total = SEGS_MAX * ROWS
    last = SEGS_MAX - 1

    def rows(cols):
        return pl.BlockSpec((ROWS, cols), lambda s: (last - s, 0))

    def lanes(height):
        return pl.BlockSpec((height, ROWS), lambda s: (0, last - s))

    def fixed(*shape):
        return pl.BlockSpec(shape, lambda s: (0,) * len(shape))

    seg_block = pl.BlockSpec((1, TEXT, width), lambda s: (last - s, 0, 0))
    sds = jax.ShapeDtypeStruct
    return pl.pallas_call(
        functools.partial(backward_kernel, plan, len(pieces)),
        grid=(SEGS_MAX,),
        in_specs=[scalar(), scalar(), scalar(), seg_block] + [whole()] * 2 + [remain()] * len(pieces)
        + [
            lanes(3 * width), lanes(width), pl.BlockSpec((1, 16, ROWS), lambda s: (last - s, 0, 0)),
            rows(width), rows(1), rows(hidden), rows(width), rows(1),
        ],
        out_specs=[
            rows(width), rows(width), rows(hidden), rows(width), rows(3 * width),
            fixed(8, width), fixed(blocks, block), fixed(MEM, width),
        ],
        out_shape=[
            sds((total, width), f32), sds((total, width), bf16), sds((total, hidden), bf16),
            sds((total, width), bf16), sds((total, 3 * width), bf16),
            sds((8, width), f32), sds((blocks, block), f32), sds((MEM, width), f32),
        ],
        scratch_shapes=[
            pltpu.VMEM((AUG, width), f32), pltpu.VMEM((MEM, width), f32), pltpu.VMEM((ROWS, width), f32),
            pltpu.VMEM((ROWS, width), f32), pltpu.VMEM((ROWS, width), f32),
            pltpu.VMEM((width, ROWS), bf16), pltpu.VMEM((3 * width, ROWS), f32),
        ]
        + weight_scratch(width, blocks, block)
        + [pltpu.SemaphoreType.DMA((3,))],
        compiler_params=pltpu.CompilerParams(vmem_limit_bytes=62 * 2**20),
    )(count, fill, table, out_grad, mem_grad, vec, *pieces, *saved)


class Products:
    def __init__(self, jobs, block, own, small=None, plan=None, n_pieces=0):
        self.jobs, self.block, self.own, self.small, self.plan, self.n_pieces = jobs, block, own, small, plan, n_pieces
        self.loads = []
        for _, loads, _ in jobs:
            self.loads += [load for load in loads if load not in self.loads]

    def part(self, array, load):
        kind = load[1]
        if kind is None:
            return array.shape
        if kind[0] == "rows":
            return (ROWS, array.shape[1])
        return (array.shape[0], self.block)

    def kernel(self, n_in, n_out, index_ref, table_ref, *refs):
        n_loads, n_jobs = len(self.loads), len(self.jobs)
        inputs, refs = refs[:n_in], refs[n_in:]
        pieces, refs = refs[: self.n_pieces], refs[self.n_pieces :]
        outputs, refs = refs[:n_out], refs[n_out:]
        held, refs = refs[:n_loads], refs[n_loads:]
        results, refs = refs[:n_jobs], refs[n_jobs:]
        load_sem, store_sem = refs[:2]
        weights, weight_sem = refs[2:3], refs[3:]
        step = pl.program_id(0)

        def load(n):
            source, kind = self.loads[n]
            view = inputs[source]
            if kind is not None:
                if kind[0] == "rows":
                    view = view.at[pl.ds(kind[1] * ROWS, ROWS), :]
                else:
                    place = index_ref[kind[1]] if kind[0] == "index" else kind[1]
                    view = view.at[:, pl.ds(pl.multiple_of(place * self.block, 128), self.block)]
            return pltpu.make_async_copy(view, held[n], load_sem.at[n])

        needs = [[self.loads.index(x) for x in loads] for _, loads, _ in self.jobs]
        fresh, seen = [], set()
        for need in needs:
            fresh.append([n for n in need if n not in seen])
            seen.update(need)

        def stores(n):
            kind, place, number = self.jobs[n][2]
            result, base = results[n], sum(self.store_counts[:n])
            if kind == "block":
                moves = [(result, outputs[place].at[number])]
            elif kind == "text":
                moves = []
            elif kind == "packed":
                moves = [(result, outputs[place].at[number])]
            else:
                mine, moves = index_ref[0], []
                for j in range(result.shape[0] // 2):
                    moves.append((result.at[2 * j + 1 - mine], outputs[place + 1].at[number, j]))
                    moves.append((result.at[2 * j + mine], outputs[place].at[number, j]))
            return [pltpu.make_async_copy(x, y, store_sem.at[base + m]) for m, (x, y) in enumerate(moves)]

        def shared_rows(n):
            extra = self.small[2]
            ffn = index_ref[self.jobs[n][1][1][1][1]]
            shard = results[n].shape[1] - extra
            return pltpu.make_async_copy(inputs[-1].at[:, ffn], results[n].at[:, pl.ds(shard, extra), :], store_sem.at[sum(self.store_counts) + n])

        for n, (form, _, output) in enumerate(self.jobs):

            @pl.when(step == n)
            def _():
                if n == 0:
                    for m in fresh[0]:
                        load(m).start()
                if output[0] == "packed":
                    shared_rows(n).start()
                for m in fresh[n]:
                    load(m).wait()
                for m in fresh[n + 1] if n + 1 < n_jobs else ():
                    load(m).start()
                texts = [m for m, job in enumerate(self.jobs) if job[0] == "text"]
                if texts and n == texts[0] - 1:
                    start_loads(table_ref, pieces, self.plan, weights, weight_sem[0], (0,))
                if texts and n == texts[0]:
                    wait_loads(weights, weight_sem[0], 0)

            @pl.when(step == n)
            def _():
                if form == "text":
                    seg = output[2]
                    width = weights[0].shape[1]
                    joined = held[needs[n][0]][...]
                    for c in range(3):
                        rows = held[needs[n][1 + c]][seg * ROWS : (seg + 1) * ROWS, :]
                        joined = joined + dot_nt(rows, weights[0][c * width : (c + 1) * width, :])
                    results[n][...] = joined
                    outputs[output[1]][0] = results[n][:TEXT, :]
                else:
                    left, right = needs[n]
                    value = {"tn": dot_tn, "nn": dot_nn}[form](held[left][...], held[right][...]).astype(bf16)
                    if output[0] == "packed":
                        items, rows, _ = results[n].shape
                        shard = rows - self.small[2]
                        results[n][:, :shard, :] = value.reshape(items, shard, self.block)
                        shared_rows(n).wait()
                    else:
                        results[n][...] = value.reshape(results[n].shape)

            @pl.when(step == n)
            def _():
                for copy in stores(n):
                    copy.start()
                if n == n_jobs - 1:
                    for m in range(n_jobs):
                        for copy in stores(m):
                            copy.wait()

    def __call__(self, index, arrays, out_shapes, table=None, pieces=()):
        block, own = self.block, self.own
        width = block
        scratch = [pltpu.VMEM(self.part(arrays[x[0]], x), arrays[x[0]].dtype) for x in self.loads]
        self.store_counts = []
        for form, loads, (kind, _, _) in self.jobs:
            if kind == "text":
                scratch.append(pltpu.VMEM((ROWS, width), f32))
            elif kind == "packed":
                items, _, extra, _ = self.small
                scratch.append(pltpu.VMEM((items, width // items + extra, block), bf16))
            else:
                scratch.append(pltpu.VMEM((width // own, own, block) if kind == "split" else (width, block), bf16))
            self.store_counts.append({"split": width // own, "text": 0}.get(kind, 1))
        scratch += [pltpu.SemaphoreType.DMA((len(self.loads),)), pltpu.SemaphoreType.DMA((sum(self.store_counts) + len(self.jobs),))]
        if pieces:
            scratch += [pltpu.VMEM((4 * width, width), bf16), pltpu.SemaphoreType.DMA((1,))]
        ahead = len(self.jobs) - SEGS_MAX
        text_block = pl.BlockSpec((1, TEXT, width), lambda j: (jnp.maximum(j - ahead, 0), 0, 0))
        return pl.pallas_call(
            functools.partial(self.kernel, len(arrays), len(out_shapes)),
            grid=(len(self.jobs),),
            in_specs=[scalar(), scalar()] + [remain()] * (len(arrays) + len(pieces)),
            out_specs=[remain() if dtype == bf16 else text_block for _, dtype in out_shapes],
            out_shape=[jax.ShapeDtypeStruct(shape, dtype) for shape, dtype in out_shapes],
            scratch_shapes=scratch,
            compiler_params=pltpu.CompilerParams(vmem_limit_bytes=60 * 2**20),
        )(index, index if table is None else table, *arrays, *pieces)


def text_grad_kernel(plan, n_pieces, table_ref, first_ref, gqkv_ref, *refs):
    pieces = refs[:n_pieces]
    out_ref, joined_ref, attn_ref, sems = refs[n_pieces:]
    width = attn_ref.shape[1]

    @pl.when(pl.program_id(0) == 0)
    def _():
        start_loads(table_ref, pieces, plan, (attn_ref,), sems, (0,))
        wait_loads((attn_ref,), sems, 0)

    joined = first_ref[...]
    for c in range(3):
        joined = joined + dot_nt(gqkv_ref[:, c * width : (c + 1) * width], attn_ref[c * width : (c + 1) * width, :])
    joined_ref[...] = joined
    out_ref[0] = joined_ref[:TEXT, :]


def text_grad_call(first, gqkv, table, plan, pieces):
    width = first.shape[1]

    def rows(cols):
        return pl.BlockSpec((ROWS, cols), lambda s: (s, 0))

    return pl.pallas_call(
        functools.partial(text_grad_kernel, plan, len(pieces)),
        grid=(SEGS_MAX,),
        in_specs=[scalar(), rows(width), rows(3 * width)] + [remain()] * len(pieces),
        out_specs=pl.BlockSpec((1, TEXT, width), lambda s: (s, 0, 0)),
        out_shape=jax.ShapeDtypeStruct((SEGS_MAX, TEXT, width), f32),
        scratch_shapes=[
            pltpu.VMEM((ROWS, width), f32), pltpu.VMEM((4 * width, width), bf16), pltpu.SemaphoreType.DMA((1,)),
        ],
        compiler_params=pltpu.CompilerParams(vmem_limit_bytes=48 * 2**20),
    )(table, first, gqkv, *pieces)


def swap(value, axis, size, mask):
    return lax.ppermute(value, axis, [(i, i ^ mask) for i in range(size)])


def after(value, *others):
    return lax.optimization_barrier((value, others))[0]


def moved(coords, place, mask):
    return [c[:place] + (c[place] ^ mask,) + c[place + 1 :] for c in coords]


PLANE = ((("t", 1), ("y", 2)), (("y", 2), ("t", 1)))


def gather_line(shard, sizes):
    parts = [shard] + [swap(shard, "s", sizes["s"], m) for m in range(1, sizes["s"])]
    half = sizes["s"] // 2
    return jnp.concatenate(parts[:half]), jnp.concatenate(parts[half:])


def gather_first(halves, sizes):
    out = []
    for value, ((axis, _), _) in zip(halves, PLANE):
        out.append(jnp.concatenate([value] + [swap(value, axis, sizes[axis], m) for m in range(1, sizes[axis])]))
    return tuple(out)


def gather_last(values, sizes):
    return tuple(
        tuple(swap(value, axis, sizes[axis], m) for m in range(1, sizes[axis]))
        for value, (_, (axis, _)) in zip(values, PLANE)
    )


def gather_core(first, last, sizes):
    out = []
    half = sizes["s"] // 2
    for number, (value, more, ((axis, place), (last_axis, last_place))) in enumerate(zip(first, last, PLANE)):
        coords = [(m, 0, 0, 0) for m in range(number * half, (number + 1) * half)]
        coords = sum((moved(coords, place, m) for m in range(sizes[axis])), [])
        out.append((value, coords))
        out += [(extra, moved(coords, last_place, m)) for m, extra in enumerate(more, 1)]
    return out + [
        (swap(value, "c", sizes["c"], m), moved(coords, 3, m))
        for m in range(1, sizes["c"])
        for value, coords in out
    ]


def pick(value, axis, index):
    return lax.dynamic_index_in_dim(value, index, axis, keepdims=False)


def add_low(parts):
    return sum(part.astype(f32) for part in parts).astype(bf16)


def deal(parts, place, axis, size):
    me = lax.axis_index(axis)
    return add_low([pick(p, place, me) for p in parts]), [
        add_low([pick(p, place, me ^ m) for p in parts]) for m in range(1, size)
    ]


def send(sends, axis, size):
    return [swap(part, axis, size, m) for m, part in enumerate(sends, 1)]


def body(sizes, text_rows, attn_weight, vectors, w_in, b_in, w_out, seg_count, last_fill, out_grad, mem_grad):
    width = text_rows.shape[-1]
    block = w_in.shape[1]
    n_s, n_t, n_y, n_c = (sizes[a] for a in "styc")
    n_ffn, n_items = n_y * n_c, n_s * n_t
    devices = n_ffn * n_items
    shard = width // n_items
    own = attn_weight.shape[0]
    me = {a: lax.axis_index(a) for a in "styc"}

    small = jnp.concatenate([vectors.reshape(-1), b_in.reshape(-1)])
    vec_size, small_size = vectors.size, small.size
    small_rows = -(-small_size // (width * 16)) * 16
    small = jnp.pad(small, (0, small_rows * width - small_size)).reshape(small_rows, width)
    direct = own % 16 == 0 and shard % 16 == 0

    def absolute(masks):
        return [me[a] ^ m for a, m in zip("styc", masks)]

    if direct:
        line = gather_line(jnp.concatenate([attn_weight, small]), sizes)
        first = gather_first(line, sizes)
        last = gather_last(first, sizes)
        feeds = lax.all_gather(jnp.concatenate([w_in, w_out.T]), ("s", "t", "y", "c"), axis=0, tiled=True)
        gathered = [gather_core(first, last, sizes)]
        text_rows = after(text_rows, last)
        plan, table, pieces, smalls = [], [], [], []
        for target, found in enumerate(gathered):
            for value, coords in found:
                each = value.shape[0] // len(coords)
                for j, masks in enumerate(coords):
                    s, t, y, c = absolute(masks)
                    item, ffn = s * n_t + t, y * n_c + c
                    if target == 0:
                        plan.append((len(pieces), j * each, own, 0))
                        table.append((item * n_ffn + ffn) * own)
                        smalls.append((item * n_ffn + ffn, value[j * each + own]))
                    else:
                        plan.append((len(pieces), j * each, shard, target))
                        table.append(ffn * width + item * shard)
                pieces.append(value)
        for device in range(devices):
            item, ffn = device // n_ffn, device % n_ffn
            for target in (1, 2):
                plan.append((len(pieces), (2 * device + target - 1) * shard, shard, target))
                table.append(jnp.int32(ffn * width + item * shard))
        pieces.append(feeds)
        place = jnp.stack([d for d, _ in smalls])
        rows = jnp.stack([row for _, row in smalls])
        rows = rows[jnp.argsort(place)][:, :small_size]
    else:
        def all_of(value):
            return lax.all_gather(value, ("s", "t", "y", "c"), axis=0)

        def by_block(value):
            parts = all_of(value).reshape(n_items, n_ffn, shard, block)
            return parts.transpose(1, 0, 2, 3).reshape(n_ffn * width, block)

        pieces = [all_of(attn_weight).reshape(-1, width), by_block(w_in), by_block(w_out.T)]
        plan = [(i, 0, p.shape[0], i) for i, p in enumerate(pieces)]
        table = [jnp.int32(0)] * 3
        rows = all_of(small).reshape(devices, -1)[:, :small_size]
    table = jnp.stack(table).astype(jnp.int32)
    rows = rows.astype(f32)
    vec = rows[:, :vec_size].reshape(devices, vectors.shape[0], -1).transpose(1, 0, 2).reshape(-1, width)
    bias = rows[:, vec_size:].reshape(n_items, n_ffn, -1).transpose(1, 0, 2).reshape(n_ffn, block)
    col = vec[:2].T

    (activations, memory, zl, qkv, mixed, lse, n1, r1, hl, act, slope, n2, r2) = forward_call(
        seg_count, last_fill, text_rows[0], bias, vec, col, table, plan, pieces
    )
    first_grad, gbranch, gpre, gattn, gqkv, vgrad, bgrad, gmem = backward_call(
        seg_count, last_fill, out_grad[0], mem_grad, vec,
        (qkv, mixed, lse, n1, r1, slope, n2, r2), (n_ffn, block), table, plan, pieces,
    )

    attn_plan = [entry for entry in plan if entry[3] == 0]
    attn_used = sorted({entry[0] for entry in attn_plan})
    attn_plan = [(attn_used.index(entry[0]),) + entry[1:] for entry in attn_plan]
    attn_pieces = [pieces[n] for n in attn_used]
    n_vec = vectors.shape[0]

    small_total = jnp.concatenate([vgrad, gmem])

    class Plane:
        def __init__(self, halves, names):
            self.parts, self.names = halves, [list(names)] * 2

        def deal(self, step):
            keeps, self.sends = [], []
            for n, (parts, order) in enumerate(zip(self.parts, PLANE)):
                axis = order[step][0]
                keep, sends = deal(parts, self.names[n].index(axis), axis, sizes[axis])
                keeps.append(keep)
                self.sends.append(sends)
                self.names[n] = [x for x in self.names[n] if x != axis]
            self.keeps = keeps
            return self.sends

        def swap(self, step):
            self.arrived = [
                send(sends, order[step][0], sizes[order[step][0]]) for sends, order in zip(self.sends, PLANE)
            ]

        def take(self):
            self.parts = [[keep] + more for keep, more in zip(self.keeps, self.arrived)]

        def deal_line(self):
            whole = jnp.concatenate([add_low(parts) for parts in self.parts])
            self.keeps, self.sends = deal([whole], 0, "s", n_s)
            return self.sends

        def swap_line(self):
            self.arrived = send(self.sends, "s", n_s)

        def line(self):
            return sum((x.astype(f32) for x in self.arrived), self.keeps.astype(f32))

    def s_halves(parts, place):
        return [[lax.slice_in_dim(p, n * n_s // 2, (n + 1) * n_s // 2, axis=place) for p in parts] for n in range(2)]

    if direct:
        mine = me["c"].astype(jnp.int32)
        index = jnp.stack([mine] + [n_c * y + mine for y in range(n_y)] + [n_c * y + 1 - mine for y in range(n_y)])

        def blocks_of(left, right, which, output, kind="block"):
            return [
                ("tn", ((left, None), (right, ("index", 1 + which * n_y + y))), (kind, output, y)) for y in range(n_y)
            ]

        plain = ((n_y, width, block), bf16)
        packed = ((n_y, n_items, shard + 16, block), bf16)
        dealt = [((2, width // own // 2, own, width), bf16)] * 2

        (out_send,) = Products(blocks_of(0, 1, 1, 0), block, own)(index, (gbranch, act), [plain])
        out_arrived = swap(out_send, "c", n_c, 1)
        small = jnp.concatenate(
            [
                small_total.reshape(n_vec, devices, -1).transpose(1, 0, 2).reshape(devices, -1),
                bgrad.reshape(n_ffn, n_items, -1).transpose(1, 0, 2).reshape(devices, -1),
            ],
            axis=1,
        ).astype(bf16)
        small = jnp.pad(small, ((0, 0), (0, 16 * block - small_size))).reshape(n_items, n_ffn, 16, block)
        out_keep, in_send = Products(
            blocks_of(0, 1, 0, 0) + blocks_of(2, 3, 1, 1, "packed"), block, own, small.shape
        )(index, (after(gbranch, out_send), act, hl, gpre, small), [plain, packed])

        def shaped(value):
            return value.reshape(n_y, n_s, n_t, -1, block)

        def attn_shaped(value):
            return value.reshape(2, n_t, n_y, own, width)

        out_arrived, out_keep, in_send = lax.optimization_barrier((out_arrived, out_keep, in_send))
        out = Plane(s_halves([shaped(out_keep), shaped(out_arrived)], 1), "yst")
        sends = out.deal(0)
        out.swap(0)

        in_arrived = swap(in_send, "c", n_c, 1)
        in_keep, keep_high, send_high = Products(
            blocks_of(0, 1, 0, 0, "packed")
            + [("tn", ((2, None), (3, ("column", 2))), ("split", 1, 0)), ("nn", ((4, None), (5, None)), ("split", 1, 1))],
            block, own, small.shape,
        )(index, (after(hl, sends), gpre, zl, gqkv, mixed, gattn, small), [packed] + dealt)
        out.arrived, in_arrived, in_keep, keep_high, send_high = lax.optimization_barrier(
            (out.arrived, in_arrived, in_keep, keep_high, send_high)
        )
        out.take()
        sends = out.deal(1)
        out.swap(1)
        feed = Plane(s_halves([shaped(in_keep), shaped(in_arrived)], 1), "yst")
        sends += feed.deal(0)
        feed.swap(0)
        high_arrived = swap(send_high, "c", n_c, 1)

        three = [(1, ("column", c)) for c in range(3)]
        keep_low, send_low, text_grad = Products(
            [("tn", ((0, None), three[c]), ("split", 0, c)) for c in range(2)]
            + [("text", [(2, ("rows", seg))] + three, ("text", 2, seg)) for seg in range(SEGS_MAX)],
            block, own, None, attn_plan, len(attn_pieces),
        )(index, (after(zl, sends), gqkv, first_grad), dealt + [((SEGS_MAX, TEXT, width), f32)], table, attn_pieces)
        out.arrived, feed.arrived, high_arrived, keep_low, send_low, text_grad = lax.optimization_barrier(
            (out.arrived, feed.arrived, high_arrived, keep_low, send_low, text_grad)
        )
        low_arrived = swap(send_low, "c", n_c, 1)
        out.take()
        sends = out.deal_line()
        out.swap_line()
        feed.take()
        sends += feed.deal(1)
        feed.swap(1)
        low_arrived, high_arrived, sends = lax.optimization_barrier((low_arrived, high_arrived, sends))
        last = Plane([[attn_shaped(keep_low), attn_shaped(low_arrived)], [attn_shaped(keep_high), attn_shaped(high_arrived)]], "sty")
        sends += last.deal(0)
        last.swap(0)
        text_grad = with_layout_constraint(after(text_grad, sends).transpose(1, 0, 2), Layout((0, 1, 2)))
        out.arrived, feed.arrived, last.arrived, text_grad = lax.optimization_barrier(
            (out.arrived, feed.arrived, last.arrived, text_grad)
        )
        feed.take()
        sends = feed.deal_line()
        feed.swap_line()
        last.take()
        sends += last.deal(1)
        last.swap(1)
        activations = with_layout_constraint(after(activations, sends).transpose(1, 0, 2), Layout((0, 1, 2)))
        w_out_grad = out.line().T
        feed.arrived, last.arrived, activations = lax.optimization_barrier((feed.arrived, last.arrived, activations))
        last.take()
        last.deal_line()
        last.swap_line()
        in_own = feed.line()
        w_in_grad = in_own[:shard]
        small_own = in_own[shard:].reshape(-1)[:small_size]
        vector_grad = small_own[:vec_size].reshape(vectors.shape)
        b_in_grad = small_own[vec_size:].reshape(b_in.shape)
        attn_grad = last.line()
        activations, text_grad = activations.transpose(1, 0, 2), text_grad.transpose(1, 0, 2)
    else:
        axes = ("s", "t", "y", "c")

        def scatter_block(left, right):
            total = dot_tn(left, right).astype(bf16).reshape(n_items, shard, n_ffn, block).transpose(0, 2, 1, 3)
            total = total.reshape(devices, shard, block)
            return lax.psum_scatter(total, axes, scatter_dimension=0, tiled=False).astype(f32)

        w_out_grad = scatter_block(gbranch, act).T
        w_in_grad = scatter_block(hl, gpre)
        total = [dot_tn(zl, gqkv[:, c * width : (c + 1) * width]) for c in range(3)] + [dot_nn(mixed, gattn)]
        total = jnp.concatenate(total).astype(bf16)
        attn_grad = lax.psum_scatter(total, axes, scatter_dimension=0, tiled=True).astype(f32)
        vector_grad = lax.psum_scatter(small_total, axes, scatter_dimension=1, tiled=True)
        b_total = bgrad.reshape(n_ffn, n_items, -1).transpose(1, 0, 2).reshape(devices, 1, -1)
        b_in_grad = lax.psum_scatter(b_total, axes, scatter_dimension=0, tiled=False)
        text_grad = text_grad_call(first_grad, gqkv, table, attn_plan, attn_pieces)
    return (activations[None], memory[None], text_grad[None], attn_grad, vector_grad, w_in_grad, b_in_grad, w_out_grad)


def solution(mesh):
    items, ffn = mesh.shape["items"], mesh.shape["ffn"]
    sizes = {"s": 4, "t": items // 4, "y": ffn // 2, "c": 2}
    grid = jax.sharding.Mesh(mesh.devices.reshape(tuple(sizes.values())), tuple(sizes))
    both, item, feed = P(("s", "t", "y", "c")), ("s", "t"), ("y", "c")
    last = P(None, ("s", "t", "y", "c"))
    return jax.shard_map(
        functools.partial(body, sizes),
        mesh=grid,
        in_specs=(both, both, last, P(item, feed), P(feed, item), P(feed, item), both, both, both, both),
        out_specs=(both, both, both, both, last, P(item, feed), P(feed, item), P(feed, item)),
        check_vma=False,
    )
```

```python
import functools

import jax
import jax.numpy as jnp
from jax import lax
from jax.experimental import pallas as pl
from jax.experimental.layout import Layout, with_layout_constraint
from jax.experimental.pallas import tpu as pltpu
from jax.sharding import PartitionSpec as P

HEADS = 12
HD = 64
MEM = 10
TEXT = 502
SEGS_MAX = 4
ROWS = TEXT + MEM
AUG = 16

epsilon = 1e-12
root_half = 0.7071067811865476
inv_root_tau = 0.3989422804014327
log_two = 0.6931471805599453

f32 = jnp.float32
bf16 = jnp.bfloat16
AXES = ("items", "ffn")


def dot_nn(a, b):
    return jnp.dot(a, b, preferred_element_type=f32)


def dot_nt(a, b):
    return lax.dot_general(a, b, (((1,), (1,)), ((), ())), preferred_element_type=f32)


def dot_tn(a, b):
    return lax.dot_general(a, b, (((0,), (0,)), ((), ())), preferred_element_type=f32)


def split_three(value):
    high = value.astype(bf16)
    rest = value - high.astype(f32)
    mid = rest.astype(bf16)
    last = (rest - mid.astype(f32)).astype(bf16)
    return high, mid, last


def gelu_both(pre):
    half = 0.5 * (1.0 + lax.erf(pre * root_half))
    slope = half + pre * jnp.exp(-0.5 * pre * pre) * inv_root_tau
    return pre * half, slope


def norm_rows(value):
    centered = value - jnp.mean(value, axis=-1, keepdims=True)
    inverse = lax.rsqrt(jnp.mean(centered * centered, axis=-1, keepdims=True) + epsilon)
    return centered * inverse, inverse


def norm_rows_back(upstream, normed, inverse, gain):
    scaled = upstream * gain
    return inverse * (
        scaled
        - jnp.mean(scaled, axis=-1, keepdims=True)
        - normed * jnp.mean(scaled * normed, axis=-1, keepdims=True)
    )


def fill_limit(seg, count, fill):
    return jnp.where(seg < count, jnp.where(seg == count - 1, fill, TEXT), 0)


def aug_rows(first, second):
    width = first[0].shape[1]
    row = lax.broadcasted_iota(jnp.int32, (AUG, width), 0)
    out = jnp.zeros((AUG, width), f32)
    for place, piece in enumerate(tuple(first) + tuple(second)):
        out = jnp.where(row == place, jnp.broadcast_to(piece.astype(f32), (AUG, width)), out)
    return out.astype(bf16)


def ones_three(width):
    one = jnp.ones((1, width), bf16)
    return (one, one, one)


def key_bias(limit):
    place = lax.broadcasted_iota(jnp.int32, (1, ROWS), 1)
    bias = jnp.where(place < limit, 0.0, jnp.where(place < TEXT, -1e9, log_two)).astype(f32)
    return split_three(bias)


def start_loads(table_ref, pieces, plan, targets, sems, wanted):
    for place, (piece, start, rows, target) in enumerate(plan):
        if target not in wanted:
            continue
        dest = pl.multiple_of(table_ref[place], rows)
        pltpu.make_async_copy(
            pieces[piece].at[pl.ds(start, rows), :], targets[target].at[pl.ds(dest, rows), :], sems.at[target]
        ).start()


def wait_loads(targets, sems, target):
    pltpu.make_async_copy(targets[target], targets[target], sems.at[target]).wait()


def early_kernel(plan, n_pieces, count_ref, fill_ref, table_ref, text_ref, col_ref, *refs):
    pieces = refs[:n_pieces]
    qkv_ref, mean_ref, lse_ref, z_ref, attn_ref, turned_ref, sems = refs[n_pieces:]
    seg = pl.program_id(0)
    limit = fill_limit(seg, count_ref[0], fill_ref[0])
    width = z_ref.shape[1]

    @pl.when(seg == 0)
    def _():
        start_loads(table_ref, pieces, plan, (attn_ref,), sems, (0,))
        z_ref[...] = jnp.zeros_like(z_ref)
        wait_loads((attn_ref,), sems, 0)
        for c in range(3):
            turned_ref[c * width : (c + 1) * width, :] = attn_ref[c * width : (c + 1) * width, :].T

    z_ref[:TEXT, :] = text_ref[0].astype(f32)
    zl = z_ref[...].astype(bf16)
    lane = lax.broadcasted_iota(jnp.int32, (1, ROWS), 1)
    for c in range(3):
        part = dot_nt(turned_ref[c * width : (c + 1) * width, :], zl)
        if c != 1:
            part = part + col_ref[:, c // 2 : c // 2 + 1]
        part = jnp.where(lane < TEXT, part, 0.0).astype(bf16)
        if c == 0:
            part = part * jnp.asarray(HD ** (-0.5), bf16)
        qkv_ref[c * width : (c + 1) * width, :] = part

    ones = ones_three(ROWS)
    key_aug = aug_rows(split_three(jnp.where(lane < limit, 0.0, -1e9).astype(f32)), ())
    query_aug = aug_rows(ones, ())

    def scores_of(head):
        lo = head * HD
        q_aug = jnp.concatenate([qkv_ref[lo : lo + HD, :], query_aug], axis=0)
        k_aug = jnp.concatenate([qkv_ref[width + lo : width + lo + HD, :], key_aug], axis=0)
        return dot_tn(k_aug, q_aug)

    def mix(head, peak, expo):
        lo = head * HD
        v_aug = jnp.concatenate([qkv_ref[2 * width + lo : 2 * width + lo + HD, :], query_aug], axis=0)
        both = dot_nn(v_aug, expo)
        total = both[HD : HD + 1, :]
        mean_ref[lo : lo + HD, :] = jnp.where(lane < TEXT, both[:HD, :] * (1.0 / total), 0.0).astype(bf16)
        lse_ref[0, head : head + 1, :] = jnp.where(lane < TEXT, peak + jnp.log(total), 0.0)

    lse_ref[...] = jnp.zeros_like(lse_ref)
    scores, held = scores_of(0), None
    for head in range(HEADS):
        following = scores_of(head + 1) if head + 1 < HEADS else None
        if held is not None:
            mix(head - 1, *held)
        peak = jnp.max(scores, axis=0, keepdims=True)
        held = peak, jnp.exp(scores - peak).astype(bf16)
        scores = following
    mix(HEADS - 1, *held)


def early_call(count, fill, text, col, table, plan, pieces):
    width = text.shape[-1]
    total = SEGS_MAX * ROWS

    def lanes(height):
        return pl.BlockSpec((height, ROWS), lambda s: (0, s))

    sds = jax.ShapeDtypeStruct
    return pl.pallas_call(
        functools.partial(early_kernel, plan, len(pieces)),
        grid=(SEGS_MAX,),
        in_specs=[scalar(), scalar(), scalar(), pl.BlockSpec((1, TEXT, width), lambda s: (s, 0, 0)), whole()]
        + [remain()] * len(pieces),
        out_specs=[lanes(3 * width), lanes(width), pl.BlockSpec((1, 16, ROWS), lambda s: (s, 0, 0))],
        out_shape=[sds((3 * width, total), bf16), sds((width, total), bf16), sds((SEGS_MAX, 16, ROWS), f32)],
        scratch_shapes=[
            pltpu.VMEM((ROWS, width), f32), pltpu.VMEM((4 * width, width), bf16),
            pltpu.VMEM((3 * width, width), bf16), pltpu.SemaphoreType.DMA((1,)),
        ],
        compiler_params=pltpu.CompilerParams(vmem_limit_bytes=62 * 2**20),
    )(count, fill, table, text, col, *pieces)


def forward_kernel(
    plan, n_pieces, count_ref, fill_ref, table_ref, text_ref, bin_ref, vec_ref, *refs,
):
    early, pieces, refs = refs[:3], refs[3 : 3 + n_pieces], refs[3 + n_pieces :]
    forward_segment(plan, pieces, count_ref, fill_ref, table_ref, text_ref, bin_ref, vec_ref, *early, *refs)


def forward_segment(
    plan, pieces, count_ref, fill_ref, table_ref, text_ref, bin_ref, vec_ref, text_qkv_ref, mean_ref, text_lse_ref,
    out_ref, mem_ref, zl_ref, qkv_ref, mixed_ref, lse_ref, n1_ref, r1_ref, hl_ref, act_ref,
    slope_ref, n2_ref, r2_ref,
    memory, z_ref, h_ref, acc_ref, attn_ref, win_ref, wout_ref, sems,
):
    weights = (attn_ref, win_ref, wout_ref)
    seg = pl.program_id(0)
    count, fill = count_ref[0], fill_ref[0]
    limit = fill_limit(seg, count, fill)
    width = z_ref.shape[1]

    @pl.when(seg == 0)
    def _():
        start_loads(table_ref, pieces, plan, weights, sems, (0,))
        memory[...] = jnp.zeros_like(memory)
        memory[:MEM, :] = vec_ref[8 : 8 + MEM, :]
        wait_loads(weights, sems, 0)
        start_loads(table_ref, pieces, plan, weights, sems, (1, 2))

    z_ref[:TEXT, :] = text_ref[0].astype(f32)
    z_ref[TEXT:, :] = memory[:MEM, :]
    zl_ref[...] = z_ref[...].astype(bf16)

    edge = ROWS - 128
    low = memory[...].astype(bf16)
    row = lax.broadcasted_iota(jnp.int32, (AUG, 1), 0)
    spots = lax.broadcasted_iota(jnp.int32, (AUG, 128), 1) == row + (TEXT - edge)
    spots = jnp.where(spots & (row < MEM), 1.0, 0.0).astype(bf16)
    few = []
    for c in range(3):
        part = dot_nn(low, attn_ref[c * width : (c + 1) * width, :])
        if c != 1:
            part = part + vec_ref[c // 2 : c // 2 + 1, :]
        part = jnp.where(row < MEM, part, 0.0).astype(bf16)
        if c == 0:
            part = part * jnp.asarray(HD ** (-0.5), bf16)
        few.append(part)
        rows = slice(c * width, (c + 1) * width)
        qkv_ref[rows, :edge] = text_qkv_ref[rows, :edge]
        qkv_ref[rows, edge:] = (text_qkv_ref[rows, edge:].astype(f32) + dot_tn(part, spots)).astype(bf16)

    tall = (HEADS * AUG, 1)
    tall_row = lax.broadcasted_iota(jnp.int32, tall, 0)
    its_head = (tall_row >> 4) == (lax.broadcasted_iota(jnp.int32, (1, width), 1) >> 6)
    its_row = tall_row & 15

    def by_head(value):
        value = jnp.concatenate([value.astype(f32)] * HEADS, axis=0)
        return jnp.where(its_head, value, 0.0).astype(bf16)

    q_few, k_few, v_few = (by_head(part) for part in few)

    lane = lax.broadcasted_iota(jnp.int32, (1, ROWS), 1)
    scores = dot_nn(q_few, text_qkv_ref[width : 2 * width, :]) + jnp.where(lane < limit, 0.0, -1e9)
    peak = jnp.max(scores, axis=1, keepdims=True)
    expo = jnp.exp(scores - peak)
    total = jnp.sum(expo, axis=1, keepdims=True)
    mean = dot_nt((expo / total).astype(bf16), text_qkv_ref[2 * width :, :])
    mean = jnp.sum(jnp.where(its_head, mean, 0.0).reshape(HEADS, AUG, width), axis=0).astype(bf16)
    mean_edge = mean_ref[:, edge:].astype(f32) + dot_tn(mean, spots)
    head_lane = lax.broadcasted_iota(jnp.int32, (1, AUG), 1)
    spread = jnp.where((tall_row >> 4) == head_lane, peak + jnp.log(total), 0.0)
    tall_spots = lax.broadcasted_iota(jnp.int32, (HEADS * AUG, 128), 1) == its_row + (TEXT - edge)
    tall_spots = jnp.where(tall_spots & (its_row < MEM), 1.0, 0.0).astype(bf16)
    lse_ref[0, :, :edge] = text_lse_ref[0, :, :edge]
    lse_ref[0, :, edge:] = text_lse_ref[0, :, edge:] + sum(dot_tn(piece, tall_spots) for piece in split_three(spread))

    scores = dot_nn(k_few, qkv_ref[:width, :]) + jnp.where(its_row < MEM, log_two, -1e9)
    scores = scores.reshape(HEADS, AUG, ROWS)
    text_lse = lse_ref[0, :HEADS, :]
    peak = jnp.maximum(text_lse, jnp.max(scores, axis=1))
    expo = jnp.exp(scores - peak[:, None, :])
    text_part = jnp.exp(text_lse - peak)
    total = text_part + jnp.sum(expo, axis=1)
    inverse = 1.0 / total
    lse_ref[0, :HEADS, :] = peak + jnp.log(total)
    text_part = text_part * inverse
    expo = (expo * inverse[:, None, :]).reshape(HEADS * AUG, ROWS).astype(bf16)
    extra = dot_tn(v_few, expo)
    for head in range(HEADS):
        rows = slice(head * HD, (head + 1) * HD)
        share = text_part[head : head + 1, :]
        mixed_ref[rows, :edge] = (mean_ref[rows, :edge].astype(f32) * share[:, :edge] + extra[rows, :edge]).astype(bf16)
        mixed_ref[rows, edge:] = (mean_edge[rows, :] * share[:, edge:] + extra[rows, edge:]).astype(bf16)

    first = z_ref[...] + (dot_tn(mixed_ref[...], attn_ref[3 * width :, :]) + vec_ref[2:3, :])
    normed, inverse = norm_rows(first)
    n1_ref[...] = normed.astype(bf16)
    r1_ref[...] = inverse
    h = normed * vec_ref[3:4, :] + vec_ref[4:5, :]
    h_ref[...] = h
    hl_ref[...] = h.astype(bf16)

    @pl.when(seg == 0)
    def _():
        wait_loads(weights, sems, 1)
        wait_loads(weights, sems, 2)

    blocks, block = bin_ref.shape
    for low in range(0, ROWS, ROWS // 2):
        rs = slice(low, low + ROWS // 2)
        for f in range(blocks):
            sl, cs = slice(f * width, (f + 1) * width), slice(f * block, (f + 1) * block)
            pre = dot_nn(hl_ref[rs, :], win_ref[sl, :]) + bin_ref[f : f + 1, :]
            act, slope = gelu_both(pre)
            act_ref[rs, cs] = act.astype(bf16)
            slope_ref[rs, cs] = slope.astype(bf16)
        part = dot_nt(act_ref[rs, :block], wout_ref[:width, :])
        for f in range(1, blocks):
            part += dot_nt(act_ref[rs, f * block : (f + 1) * block], wout_ref[f * width : (f + 1) * width, :])
        acc_ref[rs, :] = part

    normed, inverse = norm_rows(h_ref[...] + (acc_ref[...] + vec_ref[5:6, :]))
    n2_ref[...] = normed.astype(bf16)
    r2_ref[...] = inverse
    y = normed * vec_ref[6:7, :] + vec_ref[7:8, :]
    row = lax.broadcasted_iota(jnp.int32, (TEXT, 1), 0)
    out_ref[0] = jnp.where(row < limit, y[:TEXT, :], 0.0).astype(bf16)
    memory[:MEM, :] = jnp.where(seg < count, y[TEXT:, :], memory[:MEM, :])
    mem_ref[...] = memory[:MEM, :]


def backward_kernel(
    plan, n_pieces, count_ref, fill_ref, table_ref, grad_ref, mgrad_ref, vec_ref, *refs,
):
    pieces, refs = refs[:n_pieces], refs[n_pieces:]
    backward_segment(plan, pieces, count_ref, fill_ref, table_ref, grad_ref, mgrad_ref, vec_ref, *refs)


def backward_segment(
    plan, pieces, count_ref, fill_ref, table_ref, grad_ref, mgrad_ref, vec_ref,
    qkv_ref, mixed_ref, lse_ref, n1_ref, r1_ref, slope_ref, n2_ref, r2_ref,
    first_ref, gbranch_ref, gpre_ref, gattn_ref, gqkv_ref, vgrad_ref, bgrad_ref, gmem_ref,
    edge_ref, gm_ref, gy_ref, second_ref, acc_ref, mix_ref, cols_ref, attn_ref, win_ref, wout_ref, sems,
):
    weights = (attn_ref, win_ref, wout_ref)
    step = pl.program_id(0)
    seg = SEGS_MAX - 1 - step
    count, fill = count_ref[0], fill_ref[0]
    limit = fill_limit(seg, count, fill)
    width = gy_ref.shape[1]

    @pl.when(step == 0)
    def _():
        start_loads(table_ref, pieces, plan, weights, sems, (1, 2))
        gm_ref[...] = mgrad_ref[0]
        vgrad_ref[...] = jnp.zeros_like(vgrad_ref)
        bgrad_ref[...] = jnp.zeros_like(bgrad_ref)

    row = lax.broadcasted_iota(jnp.int32, (TEXT, 1), 0)
    gy_ref[:TEXT, :] = jnp.where(row < limit, grad_ref[0].astype(f32), 0.0)
    gy_ref[TEXT:, :] = jnp.where(seg < count, gm_ref[...], 0.0)

    def column_sum(value):
        return jnp.sum(value, axis=0, keepdims=True)

    gy = gy_ref[...]
    normed = n2_ref[...].astype(f32)
    vgrad_ref[6:7, :] += column_sum(gy * normed)
    vgrad_ref[7:8, :] += column_sum(gy)
    second = norm_rows_back(gy, normed, r2_ref[...], vec_ref[6:7, :])
    second_ref[...] = second
    gbranch_ref[...] = second.astype(bf16)
    vgrad_ref[5:6, :] += column_sum(gbranch_ref[...].astype(f32))

    @pl.when(step == 0)
    def _():
        wait_loads(weights, sems, 2)
        wait_loads(weights, sems, 1)
        start_loads(table_ref, pieces, plan, weights, sems, (0,))

    blocks, block = bgrad_ref.shape
    for f in range(blocks):
        sl = slice(f * block, (f + 1) * block)
        rows = slice(f * width, (f + 1) * width)
        hidden = dot_nn(gbranch_ref[...], wout_ref[rows, :])
        pre = (hidden * slope_ref[:, sl].astype(f32)).astype(bf16)
        gpre_ref[:, sl] = pre
        bgrad_ref[f : f + 1, :] += column_sum(pre.astype(f32))
        part = dot_nt(gpre_ref[:, sl], win_ref[rows, :])
        if f == 0:
            acc_ref[...] = part
        else:
            acc_ref[...] += part

    gh = second_ref[...] + acc_ref[...]
    normed = n1_ref[...].astype(f32)
    vgrad_ref[3:4, :] += column_sum(gh * normed)
    vgrad_ref[4:5, :] += column_sum(gh)
    first = norm_rows_back(gh, normed, r1_ref[...], vec_ref[3:4, :])
    second_ref[...] = first
    gattn_ref[...] = first.astype(bf16)
    vgrad_ref[2:3, :] += column_sum(gattn_ref[...].astype(f32))

    @pl.when(step == 0)
    def _():
        wait_loads(weights, sems, 0)

    mix_ref[...] = dot_nt(attn_ref[3 * width :, :], gattn_ref[...]).astype(bf16)

    ones = ones_three(ROWS)
    key_aug = aug_rows(key_bias(limit), ones)
    value_aug = aug_rows(ones, ())

    def maps_of(head):
        lo = head * HD
        q_h = qkv_ref[lo : lo + HD, :]
        k_h = qkv_ref[width + lo : width + lo + HD, :]
        v_h = qkv_ref[2 * width + lo : 2 * width + lo + HD, :]
        g_h = mix_ref[lo : lo + HD, :]
        inner = column_sum(g_h.astype(f32) * mixed_ref[lo : lo + HD, :].astype(f32))
        q_aug = jnp.concatenate([q_h, aug_rows(ones, split_three(-lse_ref[0, head : head + 1, :]))], axis=0)
        k_aug = jnp.concatenate([k_h, key_aug], axis=0)
        v_aug = jnp.concatenate([v_h, value_aug], axis=0)
        g_aug = jnp.concatenate([g_h, aug_rows(split_three(-inner), ())], axis=0)
        return dot_tn(q_aug, k_aug), dot_tn(g_aug, v_aug)

    def spread(head, grads, probs):
        lo = head * HD
        cols_ref[lo : lo + HD, :] = dot_nt(qkv_ref[width + lo : width + lo + HD, :], grads) * (HD ** (-0.5))
        cols_ref[width + lo : width + lo + HD, :] = dot_nn(qkv_ref[lo : lo + HD, :], grads)
        cols_ref[2 * width + lo : 2 * width + lo + HD, :] = dot_nn(mix_ref[lo : lo + HD, :], probs)

    maps = maps_of(0)
    for head in range(HEADS):
        following = maps_of(head + 1) if head + 1 < HEADS else None
        probs = jnp.exp(maps[0])
        spread(head, (probs * maps[1]).astype(bf16), probs.astype(bf16))
        maps = following

    for c in range(3):
        gqkv_ref[:, c * width : (c + 1) * width] = cols_ref[c * width : (c + 1) * width, :].T.astype(bf16)
    vgrad_ref[0:1, :] += column_sum(gqkv_ref[:, :width].astype(f32))
    vgrad_ref[1:2, :] += column_sum(gqkv_ref[:, 2 * width :].astype(f32))
    first_ref[...] = second_ref[...]
    edge = ROWS - AUG
    joined = second_ref[edge:, :]
    for c in range(3):
        joined = joined + dot_nt(gqkv_ref[edge:, c * width : (c + 1) * width], attn_ref[c * width : (c + 1) * width, :])
    edge_ref[...] = joined
    gm_ref[...] = jnp.where(seg < count, edge_ref[AUG - MEM :, :], gm_ref[...])
    gmem_ref[...] = gm_ref[...]


def whole():
    return pl.BlockSpec(memory_space=pltpu.VMEM)


def scalar():
    return pl.BlockSpec(memory_space=pltpu.SMEM)


def remain():
    return pl.BlockSpec(memory_space=pl.ANY)


def weight_scratch(width, blocks, block):
    return [
        pltpu.VMEM((4 * width, width), bf16), pltpu.VMEM((blocks * width, block), bf16),
        pltpu.VMEM((blocks * width, block), bf16),
    ]


def forward_call(count, fill, text, bias, vec, early, table, plan, pieces):
    width = text.shape[-1]
    blocks, block = bias.shape
    hidden = blocks * block
    total = SEGS_MAX * ROWS

    def rows(cols):
        return pl.BlockSpec((ROWS, cols), lambda s: (s, 0))

    def lanes(height):
        return pl.BlockSpec((height, ROWS), lambda s: (0, s))

    seg_block = pl.BlockSpec((1, TEXT, width), lambda s: (s, 0, 0))
    sds = jax.ShapeDtypeStruct
    return pl.pallas_call(
        functools.partial(forward_kernel, plan, len(pieces)),
        grid=(SEGS_MAX,),
        in_specs=[scalar(), scalar(), scalar(), seg_block] + [whole()] * 2
        + [lanes(3 * width), lanes(width), pl.BlockSpec((1, 16, ROWS), lambda s: (s, 0, 0))]
        + [remain()] * len(pieces),
        out_specs=[
            seg_block, pl.BlockSpec((MEM, width), lambda s: (0, 0)),
            rows(width), lanes(3 * width), lanes(width),
            pl.BlockSpec((1, 16, ROWS), lambda s: (s, 0, 0)),
            rows(width), rows(1), rows(width), rows(hidden), rows(hidden), rows(width), rows(1),
        ],
        out_shape=[
            sds((SEGS_MAX, TEXT, width), bf16), sds((MEM, width), f32),
            sds((total, width), bf16), sds((3 * width, total), bf16), sds((width, total), bf16),
            sds((SEGS_MAX, 16, ROWS), f32),
            sds((total, width), bf16), sds((total, 1), f32), sds((total, width), bf16),
            sds((total, hidden), bf16), sds((total, hidden), bf16), sds((total, width), bf16),
            sds((total, 1), f32),
        ],
        scratch_shapes=[
            pltpu.VMEM((AUG, width), f32), pltpu.VMEM((ROWS, width), f32),
            pltpu.VMEM((ROWS, width), f32), pltpu.VMEM((ROWS, width), f32),
        ]
        + weight_scratch(width, blocks, block)
        + [pltpu.SemaphoreType.DMA((3,))],
        compiler_params=pltpu.CompilerParams(vmem_limit_bytes=62 * 2**20),
    )(count, fill, table, text, bias, vec, *early, *pieces)


def backward_call(count, fill, out_grad, mem_grad, vec, saved, shape, table, plan, pieces):
    width = out_grad.shape[-1]
    blocks, block = shape
    hidden = blocks * block
    total = SEGS_MAX * ROWS
    last = SEGS_MAX - 1

    def rows(cols):
        return pl.BlockSpec((ROWS, cols), lambda s: (last - s, 0))

    def lanes(height):
        return pl.BlockSpec((height, ROWS), lambda s: (0, last - s))

    def fixed(*shape):
        return pl.BlockSpec(shape, lambda s: (0,) * len(shape))

    seg_block = pl.BlockSpec((1, TEXT, width), lambda s: (last - s, 0, 0))
    sds = jax.ShapeDtypeStruct
    return pl.pallas_call(
        functools.partial(backward_kernel, plan, len(pieces)),
        grid=(SEGS_MAX,),
        in_specs=[scalar(), scalar(), scalar(), seg_block] + [whole()] * 2 + [remain()] * len(pieces)
        + [
            lanes(3 * width), lanes(width), pl.BlockSpec((1, 16, ROWS), lambda s: (last - s, 0, 0)),
            rows(width), rows(1), rows(hidden), rows(width), rows(1),
        ],
        out_specs=[
            rows(width), rows(width), rows(hidden), rows(width), rows(3 * width),
            fixed(8, width), fixed(blocks, block), fixed(MEM, width),
        ],
        out_shape=[
            sds((total, width), f32), sds((total, width), bf16), sds((total, hidden), bf16),
            sds((total, width), bf16), sds((total, 3 * width), bf16),
            sds((8, width), f32), sds((blocks, block), f32), sds((MEM, width), f32),
        ],
        scratch_shapes=[
            pltpu.VMEM((AUG, width), f32), pltpu.VMEM((MEM, width), f32), pltpu.VMEM((ROWS, width), f32),
            pltpu.VMEM((ROWS, width), f32), pltpu.VMEM((ROWS, width), f32),
            pltpu.VMEM((width, ROWS), bf16), pltpu.VMEM((3 * width, ROWS), f32),
        ]
        + weight_scratch(width, blocks, block)
        + [pltpu.SemaphoreType.DMA((3,))],
        compiler_params=pltpu.CompilerParams(vmem_limit_bytes=62 * 2**20),
    )(count, fill, table, out_grad, mem_grad, vec, *pieces, *saved)


class Products:
    def __init__(self, jobs, block, own, small=None, plan=None, n_pieces=0):
        self.jobs, self.block, self.own, self.small, self.plan, self.n_pieces = jobs, block, own, small, plan, n_pieces
        self.loads = []
        for _, loads, _ in jobs:
            self.loads += [load for load in loads if load not in self.loads]

    def part(self, array, load):
        kind = load[1]
        if kind is None:
            return array.shape
        if kind[0] == "rows":
            return (ROWS, array.shape[1])
        return (array.shape[0], self.block)

    def kernel(self, n_in, n_out, index_ref, table_ref, *refs):
        n_loads, n_jobs = len(self.loads), len(self.jobs)
        inputs, refs = refs[:n_in], refs[n_in:]
        pieces, refs = refs[: self.n_pieces], refs[self.n_pieces :]
        outputs, refs = refs[:n_out], refs[n_out:]
        held, refs = refs[:n_loads], refs[n_loads:]
        results, refs = refs[:n_jobs], refs[n_jobs:]
        load_sem, store_sem = refs[:2]
        weights, weight_sem = refs[2:3], refs[3:]
        step = pl.program_id(0)

        def load(n):
            source, kind = self.loads[n]
            view = inputs[source]
            if kind is not None:
                if kind[0] == "rows":
                    view = view.at[pl.ds(kind[1] * ROWS, ROWS), :]
                else:
                    place = index_ref[kind[1]] if kind[0] == "index" else kind[1]
                    view = view.at[:, pl.ds(pl.multiple_of(place * self.block, 128), self.block)]
            return pltpu.make_async_copy(view, held[n], load_sem.at[n])

        needs = [[self.loads.index(x) for x in loads] for _, loads, _ in self.jobs]
        fresh, seen = [], set()
        for need in needs:
            fresh.append([n for n in need if n not in seen])
            seen.update(need)

        def stores(n):
            kind, place, number = self.jobs[n][2]
            result, base = results[n], sum(self.store_counts[:n])
            if kind == "block":
                moves = [(result, outputs[place].at[number])]
            elif kind == "text":
                moves = []
            elif kind == "packed":
                moves = [(result, outputs[place].at[number])]
            else:
                mine, moves = index_ref[0], []
                for j in range(result.shape[0] // 2):
                    moves.append((result.at[2 * j + 1 - mine], outputs[place + 1].at[number, j]))
                    moves.append((result.at[2 * j + mine], outputs[place].at[number, j]))
            return [pltpu.make_async_copy(x, y, store_sem.at[base + m]) for m, (x, y) in enumerate(moves)]

        def shared_rows(n):
            extra = self.small[2]
            ffn = index_ref[self.jobs[n][1][1][1][1]]
            shard = results[n].shape[1] - extra
            return pltpu.make_async_copy(inputs[-1].at[:, ffn], results[n].at[:, pl.ds(shard, extra), :], store_sem.at[sum(self.store_counts) + n])

        for n, (form, _, output) in enumerate(self.jobs):

            @pl.when(step == n)
            def _():
                if n == 0:
                    for m in fresh[0]:
                        load(m).start()
                if output[0] == "packed":
                    shared_rows(n).start()
                for m in fresh[n]:
                    load(m).wait()
                for m in fresh[n + 1] if n + 1 < n_jobs else ():
                    load(m).start()
                texts = [m for m, job in enumerate(self.jobs) if job[0] == "text"]
                if texts and n == texts[0] - 1:
                    start_loads(table_ref, pieces, self.plan, weights, weight_sem[0], (0,))
                if texts and n == texts[0]:
                    wait_loads(weights, weight_sem[0], 0)

            @pl.when(step == n)
            def _():
                if form == "text":
                    seg = output[2]
                    width = weights[0].shape[1]
                    joined = held[needs[n][0]][...]
                    for c in range(3):
                        rows = held[needs[n][1 + c]][seg * ROWS : (seg + 1) * ROWS, :]
                        joined = joined + dot_nt(rows, weights[0][c * width : (c + 1) * width, :])
                    results[n][...] = joined
                    outputs[output[1]][0] = results[n][:TEXT, :]
                else:
                    left, right = needs[n]
                    value = {"tn": dot_tn, "nn": dot_nn}[form](held[left][...], held[right][...]).astype(bf16)
                    if output[0] == "packed":
                        items, rows, _ = results[n].shape
                        shard = rows - self.small[2]
                        results[n][:, :shard, :] = value.reshape(items, shard, self.block)
                        shared_rows(n).wait()
                    else:
                        results[n][...] = value.reshape(results[n].shape)

            @pl.when(step == n)
            def _():
                for copy in stores(n):
                    copy.start()
                if n == n_jobs - 1:
                    for m in range(n_jobs):
                        for copy in stores(m):
                            copy.wait()

    def __call__(self, index, arrays, out_shapes, table=None, pieces=()):
        block, own = self.block, self.own
        width = block
        scratch = [pltpu.VMEM(self.part(arrays[x[0]], x), arrays[x[0]].dtype) for x in self.loads]
        self.store_counts = []
        for form, loads, (kind, _, _) in self.jobs:
            if kind == "text":
                scratch.append(pltpu.VMEM((ROWS, width), f32))
            elif kind == "packed":
                items, _, extra, _ = self.small
                scratch.append(pltpu.VMEM((items, width // items + extra, block), bf16))
            else:
                scratch.append(pltpu.VMEM((width // own, own, block) if kind == "split" else (width, block), bf16))
            self.store_counts.append({"split": width // own, "text": 0}.get(kind, 1))
        scratch += [pltpu.SemaphoreType.DMA((len(self.loads),)), pltpu.SemaphoreType.DMA((sum(self.store_counts) + len(self.jobs),))]
        if pieces:
            scratch += [pltpu.VMEM((4 * width, width), bf16), pltpu.SemaphoreType.DMA((1,))]
        ahead = len(self.jobs) - SEGS_MAX
        text_block = pl.BlockSpec((1, TEXT, width), lambda j: (jnp.maximum(j - ahead, 0), 0, 0))
        return pl.pallas_call(
            functools.partial(self.kernel, len(arrays), len(out_shapes)),
            grid=(len(self.jobs),),
            in_specs=[scalar(), scalar()] + [remain()] * (len(arrays) + len(pieces)),
            out_specs=[remain() if dtype == bf16 else text_block for _, dtype in out_shapes],
            out_shape=[jax.ShapeDtypeStruct(shape, dtype) for shape, dtype in out_shapes],
            scratch_shapes=scratch,
            compiler_params=pltpu.CompilerParams(vmem_limit_bytes=62 * 2**20),
        )(index, index if table is None else table, *arrays, *pieces)


def text_grad_kernel(plan, n_pieces, table_ref, first_ref, gqkv_ref, *refs):
    pieces = refs[:n_pieces]
    out_ref, joined_ref, attn_ref, sems = refs[n_pieces:]
    width = attn_ref.shape[1]

    @pl.when(pl.program_id(0) == 0)
    def _():
        start_loads(table_ref, pieces, plan, (attn_ref,), sems, (0,))
        wait_loads((attn_ref,), sems, 0)

    joined = first_ref[...]
    for c in range(3):
        joined = joined + dot_nt(gqkv_ref[:, c * width : (c + 1) * width], attn_ref[c * width : (c + 1) * width, :])
    joined_ref[...] = joined
    out_ref[0] = joined_ref[:TEXT, :]


def text_grad_call(first, gqkv, table, plan, pieces):
    width = first.shape[1]

    def rows(cols):
        return pl.BlockSpec((ROWS, cols), lambda s: (s, 0))

    return pl.pallas_call(
        functools.partial(text_grad_kernel, plan, len(pieces)),
        grid=(SEGS_MAX,),
        in_specs=[scalar(), rows(width), rows(3 * width)] + [remain()] * len(pieces),
        out_specs=pl.BlockSpec((1, TEXT, width), lambda s: (s, 0, 0)),
        out_shape=jax.ShapeDtypeStruct((SEGS_MAX, TEXT, width), f32),
        scratch_shapes=[
            pltpu.VMEM((ROWS, width), f32), pltpu.VMEM((4 * width, width), bf16), pltpu.SemaphoreType.DMA((1,)),
        ],
        compiler_params=pltpu.CompilerParams(vmem_limit_bytes=62 * 2**20),
    )(table, first, gqkv, *pieces)


def deal_kernel(outputs, places, n_in, n_out, index_ref, *refs):
    inputs, refs = refs[:n_in], refs[n_in:]
    outs, refs = refs[:n_out], refs[n_out:]
    load_sem, store_sem = refs[-2:]
    held = list(refs[:-2])
    results = held[-len(outputs) :]

    def view(array, indices):
        found = []
        for index in indices:
            if index is None:
                found.append(slice(None))
            elif isinstance(index, int):
                found.append(index)
            elif index[0] == "at":
                found.append(index_ref[index[1]] + index[2])
            else:
                found.append(pl.ds(index[0], index[1] - index[0]))
        return inputs[array].at[tuple(found)]

    waits, number = [], 0
    for _, views in outputs:
        waits.append([])
        for item in views:
            target, sem = held[number], load_sem.at[number]
            number += 1
            one = pltpu.make_async_copy(view(*item[:2]), target, sem)
            if len(item) == 2:
                one.start()
            else:
                (other, which) = item[2:]
                two = pltpu.make_async_copy(view(*other), target, sem)
                pl.when(index_ref[which] == 0)(one.start)
                pl.when(index_ref[which] != 0)(two.start)
            waits[-1].append((one, target))
    stores = []
    for n, items in enumerate(waits):
        total = None
        for copy, target in items:
            copy.wait()
            part = target[...].astype(f32)
            total = part if total is None else total + part
        results[n][...] = total.astype(bf16)
        out, first = places[n]
        target = outs[out] if first is None else outs[out].at[pl.ds(first, results[n].shape[0]), :]
        stores.append(pltpu.make_async_copy(results[n], target, store_sem.at[n]))
        stores[-1].start()
    for copy in stores:
        copy.wait()


def deal(index, outputs):
    arrays, places, shapes, flat = [], [], [], []
    for n, output in enumerate(outputs):
        if isinstance(output, list):
            first = 0
            for part in output:
                places.append((n, first))
                first += part[0][0]
                flat.append(part)
            shapes.append((first,) + output[0][0][1:])
        else:
            places.append((n, None))
            flat.append(output)
            shapes.append(output[0])
    outputs = flat

    def place(array):
        for n, known in enumerate(arrays):
            if known is array:
                return n
        arrays.append(array)
        return len(arrays) - 1

    plain = []
    for shape, views in outputs:
        plain.append((shape, [
            (place(v[0]), v[1]) if len(v) == 2 else (place(v[0]), v[1], (place(v[2][0]), v[2][1]), v[3]) for v in views
        ]))
    scratch = [pltpu.VMEM(shape, bf16) for shape, views in plain for _ in views]
    n_loads = len(scratch)
    scratch += [pltpu.VMEM(shape, bf16) for shape, _ in plain]
    scratch += [pltpu.SemaphoreType.DMA((n_loads,)), pltpu.SemaphoreType.DMA((len(plain),))]
    return pl.pallas_call(
        functools.partial(deal_kernel, plain, places, len(arrays), len(shapes)),
        in_specs=[scalar()] + [remain()] * len(arrays),
        out_specs=[remain()] * len(shapes),
        out_shape=[jax.ShapeDtypeStruct(shape, bf16) for shape in shapes],
        scratch_shapes=scratch,
        compiler_params=pltpu.CompilerParams(vmem_limit_bytes=62 * 2**20),
    )(index, *arrays)


class Piece:
    MINE = {"t": 4, "y": 6}

    def __init__(self, halves):
        self.halves = halves
        self.shard = halves[0][0][0].shape[-2:]

    def views(self, half, chosen):
        out = []
        for array, names, first in self.halves[half]:
            at = []
            for name in names:
                if name in chosen:
                    at.append(chosen[name])
                elif name == "s":
                    at.append((first, first + 2))
                else:
                    at.append(None)
            out.append((array, tuple(at)))
        return out

    def plane(self, step):
        outputs, self.names = [], []
        for half, order in enumerate(PLANE):
            axis = order[step][0]
            chosen = {axis: ("at", self.MINE[axis] + 1, 0)}
            if step == 1:
                chosen[order[0][0]] = ("at", self.MINE[order[0][0]], 0)
            names = [n for n in self.halves[half][0][1] if n not in chosen]
            outputs.append((tuple(2 for _ in names) + self.shard, self.views(half, chosen)))
            self.names.append(names)
        return outputs

    def swap_plane(self, step, sends):
        self.arrived = [swap(x, order[step][0], 2, 1) for x, order in zip(sends, PLANE)]

    def take(self):
        for half, (value, names) in enumerate(zip(self.arrived, self.names)):
            self.halves[half] = self.halves[half] + [(value, names, 0)]

    def line(self):
        outputs = []
        for mask in range(4):
            views = []
            here = {"t": ("at", 4, 0), "y": ("at", 6, 0)}
            for (a, names, first), (b, other_names, other_first) in zip(*self.halves):
                def at(names, first):
                    return tuple(("at", 12 + mask, first) if n == "s" else here[n] for n in names)
                views.append((a, at(names, first), (b, at(other_names, other_first)), 8 + mask))
            outputs.append((self.shard, views))
        return outputs

    def total(self, kept, arrived):
        return sum(x.astype(f32) for x in [kept] + arrived)


def swap(value, axis, size, mask):
    return lax.ppermute(value, axis, [(i, i ^ mask) for i in range(size)])


def after(value, *others):
    return lax.optimization_barrier((value, others))[0]


def moved(coords, place, mask):
    return [c[:place] + (c[place] ^ mask,) + c[place + 1 :] for c in coords]


PLANE = ((("t", 1), ("y", 2)), (("y", 2), ("t", 1)))


def gather_line(shard, sizes, beside):
    parts = [swap(shard, "s", sizes["s"], m) for m in range(1, sizes["s"])]
    parts, beside = lax.optimization_barrier((parts, beside))
    parts = [shard] + parts
    half = sizes["s"] // 2
    return (jnp.concatenate(parts[:half]), jnp.concatenate(parts[half:])), beside


def gather_first(halves, sizes, beside):
    arrived = []
    for value, ((axis, _), _) in zip(halves, PLANE):
        arrived.append([swap(value, axis, sizes[axis], m) for m in range(1, sizes[axis])])
    arrived, beside = lax.optimization_barrier((arrived, beside))
    return tuple(jnp.concatenate([value] + more) for value, more in zip(halves, arrived)), beside


def gather_last(values, sizes):
    return tuple(
        tuple(swap(value, axis, sizes[axis], m) for m in range(1, sizes[axis]))
        for value, (_, (axis, _)) in zip(values, PLANE)
    )


def gather_core(first, last, sizes):
    out = []
    half = sizes["s"] // 2
    for number, (value, more, ((axis, place), (last_axis, last_place))) in enumerate(zip(first, last, PLANE)):
        coords = [(m, 0, 0, 0) for m in range(number * half, (number + 1) * half)]
        coords = sum((moved(coords, place, m) for m in range(sizes[axis])), [])
        out.append((value, coords))
        out += [(extra, moved(coords, last_place, m)) for m, extra in enumerate(more, 1)]
    return out + [
        (swap(value, "c", sizes["c"], m), moved(coords, 3, m))
        for m in range(1, sizes["c"])
        for value, coords in out
    ]


def pick(value, axis, index):
    return lax.dynamic_index_in_dim(value, index, axis, keepdims=False)


def body(sizes, text_rows, attn_weight, vectors, w_in, b_in, w_out, seg_count, last_fill, out_grad, mem_grad):
    width = text_rows.shape[-1]
    block = w_in.shape[1]
    n_s, n_t, n_y, n_c = (sizes[a] for a in "styc")
    n_ffn, n_items = n_y * n_c, n_s * n_t
    devices = n_ffn * n_items
    shard = width // n_items
    own = attn_weight.shape[0]
    me = {a: lax.axis_index(a) for a in "styc"}

    small = jnp.concatenate([vectors.reshape(-1), b_in.reshape(-1)])
    vec_size, small_size = vectors.size, small.size
    small_rows = -(-small_size // (width * 16)) * 16
    small = jnp.pad(small, (0, small_rows * width - small_size)).reshape(small_rows, width)
    direct = own % 16 == 0 and shard % 16 == 0 and (n_s, n_t, n_y, n_c) == (4, 2, 2, 2)

    def absolute(masks):
        return [me[a] ^ m for a, m in zip("styc", masks)]

    if direct:
        text = with_layout_constraint(text_rows[0], Layout((0, 1, 2)))
        grads = with_layout_constraint(out_grad[0], Layout((0, 1, 2)))
        line, text = gather_line(jnp.concatenate([attn_weight, small]), sizes, text)
        first, grads = gather_first(line, sizes, grads)
        text_rows, out_grad = text[None], grads[None]
        last = gather_last(first, sizes)
        feeds = lax.all_gather(jnp.concatenate([w_in, w_out.T]), ("s", "t", "y", "c"), axis=0, tiled=True)
        gathered = [gather_core(first, last, sizes)]
        plan, table, pieces, smalls = [], [], [], []
        for target, found in enumerate(gathered):
            for value, coords in found:
                each = value.shape[0] // len(coords)
                for j, masks in enumerate(coords):
                    s, t, y, c = absolute(masks)
                    item, ffn = s * n_t + t, y * n_c + c
                    if target == 0:
                        plan.append((len(pieces), j * each, own, 0))
                        table.append((item * n_ffn + ffn) * own)
                        smalls.append((item * n_ffn + ffn, value[j * each + own]))
                    else:
                        plan.append((len(pieces), j * each, shard, target))
                        table.append(ffn * width + item * shard)
                pieces.append(value)
        for device in range(devices):
            item, ffn = device // n_ffn, device % n_ffn
            for target in (1, 2):
                plan.append((len(pieces), (2 * device + target - 1) * shard, shard, target))
                table.append(jnp.int32(ffn * width + item * shard))
        pieces.append(feeds)
        place = jnp.stack([d for d, _ in smalls])
        rows = jnp.stack([row for _, row in smalls])
        rows = rows[jnp.argsort(place)][:, :small_size]
    else:
        def all_of(value):
            return lax.all_gather(value, ("s", "t", "y", "c"), axis=0)

        def by_block(value):
            parts = all_of(value).reshape(n_items, n_ffn, shard, block)
            return parts.transpose(1, 0, 2, 3).reshape(n_ffn * width, block)

        pieces = [all_of(attn_weight).reshape(-1, width), by_block(w_in), by_block(w_out.T)]
        plan = [(i, 0, p.shape[0], i) for i, p in enumerate(pieces)]
        table = [jnp.int32(0)] * 3
        rows = all_of(small).reshape(devices, -1)[:, :small_size]
    table = jnp.stack(table).astype(jnp.int32)
    rows = rows.astype(f32)
    vec = rows[:, :vec_size].reshape(devices, vectors.shape[0], -1).transpose(1, 0, 2).reshape(-1, width)
    bias = rows[:, vec_size:].reshape(n_items, n_ffn, -1).transpose(1, 0, 2).reshape(n_ffn, block)
    col = vec[:2].T

    attn_plan = [entry for entry in plan if entry[3] == 0]
    attn_used = sorted({entry[0] for entry in attn_plan})
    attn_plan = [(attn_used.index(entry[0]),) + entry[1:] for entry in attn_plan]
    attn_pieces = [pieces[n] for n in attn_used]
    early = early_call(seg_count, last_fill, text_rows[0], col, table, attn_plan, attn_pieces)

    (activations, memory, zl, qkv, mixed, lse, n1, r1, hl, act, slope, n2, r2) = forward_call(
        seg_count, last_fill, text_rows[0], bias, vec, early, table, plan, pieces
    )
    first_grad, gbranch, gpre, gattn, gqkv, vgrad, bgrad, gmem = backward_call(
        seg_count, last_fill, out_grad[0], mem_grad, vec,
        (qkv, mixed, lse, n1, r1, slope, n2, r2), (n_ffn, block), table, plan, pieces,
    )

    n_vec = vectors.shape[0]

    small_total = jnp.concatenate([vgrad, gmem])

    if direct:
        mine = me["c"].astype(jnp.int32)
        index = jnp.stack([mine] + [n_c * y + mine for y in range(n_y)] + [n_c * y + 1 - mine for y in range(n_y)])

        def blocks_of(left, right, which, output, kind="block"):
            return [
                ("tn", ((left, None), (right, ("index", 1 + which * n_y + y))), (kind, output, y)) for y in range(n_y)
            ]

        plain = ((n_y, width, block), bf16)
        packed = ((n_y, n_items, shard + 16, block), bf16)
        dealt = [((4, width // own // 2, own, width), bf16)] * 2

        (out_send,) = Products(blocks_of(0, 1, 1, 0), block, own)(index, (gbranch, act), [plain])
        out_arrived = swap(out_send, "c", n_c, 1)
        small = jnp.concatenate(
            [
                small_total.reshape(n_vec, devices, -1).transpose(1, 0, 2).reshape(devices, -1),
                bgrad.reshape(n_ffn, n_items, -1).transpose(1, 0, 2).reshape(devices, -1),
            ],
            axis=1,
        ).astype(bf16)
        small = jnp.pad(small, ((0, 0), (0, 16 * block - small_size))).reshape(n_items, n_ffn, 16, block)
        out_keep, in_send = Products(
            blocks_of(0, 1, 0, 0) + blocks_of(2, 3, 1, 1, "packed"), block, own, small.shape
        )(index, (after(gbranch, out_send), act, hl, gpre, small), [plain, packed])

        def shaped(value):
            return value.reshape(n_y, n_s, n_t, -1, block)

        def attn_shaped(value):
            return value.reshape(n_s, n_t, n_y, own, width)

        out_arrived, out_keep, in_send = lax.optimization_barrier((out_arrived, out_keep, in_send))
        lines = [me["s"] ^ m for m in range(4)]
        grid_index = jnp.stack(
            lines + [me["t"], me["t"] ^ 1, me["y"], me["y"] ^ 1] + [x // 2 for x in lines] + [x % 2 for x in lines]
        ).astype(jnp.int32)

        def deal_all(*groups):
            found, out = deal(grid_index, sum(groups, [])), []
            for group in groups:
                out.append(found[: len(group)])
                found = found[len(group) :]
            return out

        out = Piece([[(shaped(x), "yst", 2 * n) for x in (out_keep, out_arrived)] for n in range(2)])
        (sends,) = deal_all(out.plane(0))
        out.swap_plane(0, sends)
        in_arrived = swap(in_send, "c", n_c, 1)
        in_keep, attn_keep, attn_send = Products(
            blocks_of(0, 1, 0, 0, "packed")
            + [("tn", ((2, None), (3, ("column", c))), ("split", 1, c)) for c in range(3)]
            + [("nn", ((4, None), (5, None)), ("split", 1, 3))],
            block, own, small.shape,
        )(index, (after(hl, sends), gpre, zl, gqkv, mixed, gattn, small), [packed] + dealt)
        out.arrived, in_arrived, in_keep, attn_keep, attn_send = lax.optimization_barrier(
            (out.arrived, in_arrived, in_keep, attn_keep, attn_send)
        )

        out.take()
        feed = Piece([[(shaped(x), "yst", 2 * n) for x in (in_keep, in_arrived)] for n in range(2)])
        sends, more = deal_all(out.plane(1), feed.plane(0))
        out.swap_plane(1, sends)
        feed.swap_plane(0, more)
        attn_arrived = swap(attn_send, "c", n_c, 1)
        text_grad = text_grad_call(after(first_grad, sends, more), gqkv, table, attn_plan, attn_pieces)
        out.arrived, feed.arrived, attn_arrived, text_grad = lax.optimization_barrier(
            (out.arrived, feed.arrived, attn_arrived, text_grad)
        )

        out.take()
        feed.take()
        last = Piece([[(attn_shaped(x), "sty", 2 * n) for x in (attn_keep, attn_arrived)] for n in range(2)])
        out_line = out.line()
        more, lasts, (out_kept, out_two) = deal_all(feed.plane(1), last.plane(0), [out_line[0], out_line[2]])
        last.swap_plane(0, lasts)
        feed.swap_plane(1, more)
        out_two = swap(out_two, "s", 4, 2)
        text_grad = with_layout_constraint(after(text_grad, more).transpose(1, 0, 2), Layout((0, 1, 2)))
        out_two, feed.arrived, last.arrived, text_grad = lax.optimization_barrier(
            (out_two, feed.arrived, last.arrived, text_grad)
        )

        feed.take()
        last.take()
        in_line = feed.line()
        more, (in_kept, in_two, one, three) = deal_all(
            last.plane(1), [in_line[0], in_line[2], [out_line[1], in_line[1]], [out_line[3], in_line[3]]]
        )
        last.swap_plane(1, more)
        one, three, in_two = swap(one, "s", 4, 1), swap(three, "s", 4, 3), swap(in_two, "s", 4, 2)
        activations = with_layout_constraint(after(activations, more).transpose(1, 0, 2), Layout((0, 1, 2)))
        one, three, in_two, last.arrived, activations = lax.optimization_barrier(
            (one, three, in_two, last.arrived, activations)
        )

        last.take()
        attn_kept, *lines = deal_all(last.line())[0]
        lines = [swap(part, "s", 4, m) for m, part in enumerate(lines, 1)]
        w_out_grad = out.total(out_kept, [one[:shard], out_two, three[:shard]]).T
        in_own = feed.total(in_kept, [one[shard:], in_two, three[shard:]])
        w_in_grad = in_own[:shard]
        small_own = in_own[shard:].reshape(-1)[:small_size]
        vector_grad = small_own[:vec_size].reshape(vectors.shape)
        b_in_grad = small_own[vec_size:].reshape(b_in.shape)
        attn_grad = last.total(attn_kept, lines)
        activations, text_grad = activations.transpose(1, 0, 2), text_grad.transpose(1, 0, 2)
    else:
        axes = ("s", "t", "y", "c")

        def scatter_block(left, right):
            total = dot_tn(left, right).astype(bf16).reshape(n_items, shard, n_ffn, block).transpose(0, 2, 1, 3)
            total = total.reshape(devices, shard, block)
            return lax.psum_scatter(total, axes, scatter_dimension=0, tiled=False).astype(f32)

        w_out_grad = scatter_block(gbranch, act).T
        w_in_grad = scatter_block(hl, gpre)
        total = [dot_tn(zl, gqkv[:, c * width : (c + 1) * width]) for c in range(3)] + [dot_nn(mixed, gattn)]
        total = jnp.concatenate(total).astype(bf16)
        attn_grad = lax.psum_scatter(total, axes, scatter_dimension=0, tiled=True).astype(f32)
        vector_grad = lax.psum_scatter(small_total, axes, scatter_dimension=1, tiled=True)
        b_total = bgrad.reshape(n_ffn, n_items, -1).transpose(1, 0, 2).reshape(devices, 1, -1)
        b_in_grad = lax.psum_scatter(b_total, axes, scatter_dimension=0, tiled=False)
        text_grad = text_grad_call(first_grad, gqkv, table, attn_plan, attn_pieces)
    return (activations[None], memory[None], text_grad[None], attn_grad, vector_grad, w_in_grad, b_in_grad, w_out_grad)


def solution(mesh):
    items, ffn = mesh.shape["items"], mesh.shape["ffn"]
    sizes = {"s": 4, "t": items // 4, "y": ffn // 2, "c": 2}
    grid = jax.sharding.Mesh(mesh.devices.reshape(tuple(sizes.values())), tuple(sizes))
    both, item, feed = P(("s", "t", "y", "c")), ("s", "t"), ("y", "c")
    last = P(None, ("s", "t", "y", "c"))
    return jax.shard_map(
        functools.partial(body, sizes),
        mesh=grid,
        in_specs=(both, both, last, P(item, feed), P(feed, item), P(feed, item), both, both, both, both),
        out_specs=(both, both, both, both, last, P(item, feed), P(feed, item), P(feed, item)),
        check_vma=False,
    )
```

```python
import functools

import jax
import jax.numpy as jnp
from jax import lax
from jax.experimental import pallas as pl
from jax.experimental.layout import Layout, with_layout_constraint
from jax.experimental.pallas import tpu as pltpu
from jax.sharding import PartitionSpec as P

HEADS = 12
HD = 64
MEM = 10
TEXT = 502
SEGS_MAX = 4
ROWS = TEXT + MEM
AUG = 16

epsilon = 1e-12
root_half = 0.7071067811865476
inv_root_tau = 0.3989422804014327
log_two = 0.6931471805599453

f32 = jnp.float32
bf16 = jnp.bfloat16
AXES = ("items", "ffn")


def dot_nn(a, b):
    return jnp.dot(a, b, preferred_element_type=f32)


def dot_nt(a, b):
    return lax.dot_general(a, b, (((1,), (1,)), ((), ())), preferred_element_type=f32)


def dot_tn(a, b):
    return lax.dot_general(a, b, (((0,), (0,)), ((), ())), preferred_element_type=f32)


def split_three(value):
    high = value.astype(bf16)
    rest = value - high.astype(f32)
    mid = rest.astype(bf16)
    last = (rest - mid.astype(f32)).astype(bf16)
    return high, mid, last


def gelu_both(pre):
    half = 0.5 * (1.0 + lax.erf(pre * root_half))
    slope = half + pre * jnp.exp(-0.5 * pre * pre) * inv_root_tau
    return pre * half, slope


def norm_rows(value):
    centered = value - jnp.mean(value, axis=-1, keepdims=True)
    inverse = lax.rsqrt(jnp.mean(centered * centered, axis=-1, keepdims=True) + epsilon)
    return centered * inverse, inverse


def norm_rows_back(upstream, normed, inverse, gain):
    scaled = upstream * gain
    return inverse * (
        scaled
        - jnp.mean(scaled, axis=-1, keepdims=True)
        - normed * jnp.mean(scaled * normed, axis=-1, keepdims=True)
    )


def fill_limit(seg, count, fill):
    return jnp.where(seg < count, jnp.where(seg == count - 1, fill, TEXT), 0)


def aug_rows(first, second):
    width = first[0].shape[1]
    row = lax.broadcasted_iota(jnp.int32, (AUG, width), 0)
    out = jnp.zeros((AUG, width), f32)
    for place, piece in enumerate(tuple(first) + tuple(second)):
        out = jnp.where(row == place, jnp.broadcast_to(piece.astype(f32), (AUG, width)), out)
    return out.astype(bf16)


def ones_three(width):
    one = jnp.ones((1, width), bf16)
    return (one, one, one)


def key_bias(limit):
    place = lax.broadcasted_iota(jnp.int32, (1, ROWS), 1)
    bias = jnp.where(place < limit, 0.0, jnp.where(place < TEXT, -1e9, log_two)).astype(f32)
    return split_three(bias)


def start_loads(table_ref, pieces, plan, targets, sems, wanted):
    for place, (piece, start, rows, target) in enumerate(plan):
        if target not in wanted:
            continue
        dest = pl.multiple_of(table_ref[place], rows)
        pltpu.make_async_copy(
            pieces[piece].at[pl.ds(start, rows), :], targets[target].at[pl.ds(dest, rows), :], sems.at[target]
        ).start()


def wait_loads(targets, sems, target):
    pltpu.make_async_copy(targets[target], targets[target], sems.at[target]).wait()


def early_kernel(plan, n_pieces, count_ref, fill_ref, table_ref, text_ref, col_ref, *refs):
    pieces = refs[:n_pieces]
    qkv_ref, mean_ref, lse_ref, z_ref, attn_ref, turned_ref, sems = refs[n_pieces:]
    seg = pl.program_id(0)
    limit = fill_limit(seg, count_ref[0], fill_ref[0])
    width = z_ref.shape[1]

    @pl.when(seg == 0)
    def _():
        start_loads(table_ref, pieces, plan, (attn_ref,), sems, (0,))
        z_ref[...] = jnp.zeros_like(z_ref)
        wait_loads((attn_ref,), sems, 0)
        for c in range(3):
            turned_ref[c * width : (c + 1) * width, :] = attn_ref[c * width : (c + 1) * width, :].T

    z_ref[:TEXT, :] = text_ref[0].astype(f32)
    zl = z_ref[...].astype(bf16)
    lane = lax.broadcasted_iota(jnp.int32, (1, ROWS), 1)
    for c in range(3):
        part = dot_nt(turned_ref[c * width : (c + 1) * width, :], zl)
        if c != 1:
            part = part + col_ref[:, c // 2 : c // 2 + 1]
        part = jnp.where(lane < TEXT, part, 0.0).astype(bf16)
        if c == 0:
            part = part * jnp.asarray(HD ** (-0.5), bf16)
        qkv_ref[c * width : (c + 1) * width, :] = part

    ones = ones_three(ROWS)
    key_aug = aug_rows(split_three(jnp.where(lane < limit, 0.0, -1e9).astype(f32)), ())
    query_aug = aug_rows(ones, ())

    def scores_of(head):
        lo = head * HD
        q_aug = jnp.concatenate([qkv_ref[lo : lo + HD, :], query_aug], axis=0)
        k_aug = jnp.concatenate([qkv_ref[width + lo : width + lo + HD, :], key_aug], axis=0)
        return dot_tn(k_aug, q_aug)

    def mix(head, peak, expo):
        lo = head * HD
        v_aug = jnp.concatenate([qkv_ref[2 * width + lo : 2 * width + lo + HD, :], query_aug], axis=0)
        both = dot_nn(v_aug, expo)
        total = both[HD : HD + 1, :]
        mean_ref[lo : lo + HD, :] = jnp.where(lane < TEXT, both[:HD, :] * (1.0 / total), 0.0).astype(bf16)
        lse_ref[0, head : head + 1, :] = jnp.where(lane < TEXT, peak + jnp.log(total), 0.0)

    lse_ref[...] = jnp.zeros_like(lse_ref)
    scores, held = scores_of(0), None
    for head in range(HEADS):
        following = scores_of(head + 1) if head + 1 < HEADS else None
        if held is not None:
            mix(head - 1, *held)
        peak = jnp.max(scores, axis=0, keepdims=True)
        held = peak, jnp.exp(scores - peak).astype(bf16)
        scores = following
    mix(HEADS - 1, *held)


def early_call(count, fill, text, col, table, plan, pieces):
    width = text.shape[-1]
    total = SEGS_MAX * ROWS

    def lanes(height):
        return pl.BlockSpec((height, ROWS), lambda s: (0, s))

    sds = jax.ShapeDtypeStruct
    return pl.pallas_call(
        functools.partial(early_kernel, plan, len(pieces)),
        grid=(SEGS_MAX,),
        in_specs=[scalar(), scalar(), scalar(), pl.BlockSpec((1, TEXT, width), lambda s: (s, 0, 0)), whole()]
        + [remain()] * len(pieces),
        out_specs=[lanes(3 * width), lanes(width), pl.BlockSpec((1, 16, ROWS), lambda s: (s, 0, 0))],
        out_shape=[sds((3 * width, total), bf16), sds((width, total), bf16), sds((SEGS_MAX, 16, ROWS), f32)],
        scratch_shapes=[
            pltpu.VMEM((ROWS, width), f32), pltpu.VMEM((4 * width, width), bf16),
            pltpu.VMEM((3 * width, width), bf16), pltpu.SemaphoreType.DMA((1,)),
        ],
        compiler_params=pltpu.CompilerParams(vmem_limit_bytes=62 * 2**20),
    )(count, fill, table, text, col, *pieces)


def forward_kernel(
    plan, n_pieces, count_ref, fill_ref, table_ref, text_ref, bin_ref, vec_ref, *refs,
):
    early, pieces, refs = refs[:3], refs[3 : 3 + n_pieces], refs[3 + n_pieces :]
    forward_segment(plan, pieces, count_ref, fill_ref, table_ref, text_ref, bin_ref, vec_ref, *early, *refs)


def forward_segment(
    plan, pieces, count_ref, fill_ref, table_ref, text_ref, bin_ref, vec_ref, text_qkv_ref, mean_ref, text_lse_ref,
    out_ref, mem_ref, zl_ref, qkv_ref, mixed_ref, lse_ref, n1_ref, r1_ref, hl_ref, act_ref,
    slope_ref, n2_ref, r2_ref,
    memory, z_ref, h_ref, acc_ref, attn_ref, win_ref, wout_ref, sems,
):
    weights = (attn_ref, win_ref, wout_ref)
    seg = pl.program_id(0)
    count, fill = count_ref[0], fill_ref[0]
    limit = fill_limit(seg, count, fill)
    width = z_ref.shape[1]

    @pl.when(seg == 0)
    def _():
        start_loads(table_ref, pieces, plan, weights, sems, (0,))
        memory[...] = jnp.zeros_like(memory)
        memory[:MEM, :] = vec_ref[8 : 8 + MEM, :]
        wait_loads(weights, sems, 0)
        start_loads(table_ref, pieces, plan, weights, sems, (1, 2))

    z_ref[:TEXT, :] = text_ref[0].astype(f32)
    z_ref[TEXT:, :] = memory[:MEM, :]
    zl_ref[...] = z_ref[...].astype(bf16)

    edge = ROWS - 128
    low = memory[...].astype(bf16)
    row = lax.broadcasted_iota(jnp.int32, (AUG, 1), 0)
    spots = lax.broadcasted_iota(jnp.int32, (AUG, 128), 1) == row + (TEXT - edge)
    spots = jnp.where(spots & (row < MEM), 1.0, 0.0).astype(bf16)
    few = []
    for c in range(3):
        part = dot_nn(low, attn_ref[c * width : (c + 1) * width, :])
        if c != 1:
            part = part + vec_ref[c // 2 : c // 2 + 1, :]
        part = jnp.where(row < MEM, part, 0.0).astype(bf16)
        if c == 0:
            part = part * jnp.asarray(HD ** (-0.5), bf16)
        few.append(part)
        rows = slice(c * width, (c + 1) * width)
        qkv_ref[rows, :edge] = text_qkv_ref[rows, :edge]
        qkv_ref[rows, edge:] = (text_qkv_ref[rows, edge:].astype(f32) + dot_tn(part, spots)).astype(bf16)

    tall = (HEADS * AUG, 1)
    tall_row = lax.broadcasted_iota(jnp.int32, tall, 0)
    its_head = (tall_row >> 4) == (lax.broadcasted_iota(jnp.int32, (1, width), 1) >> 6)
    its_row = tall_row & 15

    def by_head(value):
        value = jnp.concatenate([value.astype(f32)] * HEADS, axis=0)
        return jnp.where(its_head, value, 0.0).astype(bf16)

    q_few, k_few, v_few = (by_head(part) for part in few)

    lane = lax.broadcasted_iota(jnp.int32, (1, ROWS), 1)
    scores = dot_nn(q_few, text_qkv_ref[width : 2 * width, :]) + jnp.where(lane < limit, 0.0, -1e9)
    peak = jnp.max(scores, axis=1, keepdims=True)
    expo = jnp.exp(scores - peak)
    total = jnp.sum(expo, axis=1, keepdims=True)
    mean = dot_nt((expo / total).astype(bf16), text_qkv_ref[2 * width :, :])
    mean = jnp.sum(jnp.where(its_head, mean, 0.0).reshape(HEADS, AUG, width), axis=0).astype(bf16)
    mean_edge = mean_ref[:, edge:].astype(f32) + dot_tn(mean, spots)
    head_lane = lax.broadcasted_iota(jnp.int32, (1, AUG), 1)
    spread = jnp.where((tall_row >> 4) == head_lane, peak + jnp.log(total), 0.0)
    tall_spots = lax.broadcasted_iota(jnp.int32, (HEADS * AUG, 128), 1) == its_row + (TEXT - edge)
    tall_spots = jnp.where(tall_spots & (its_row < MEM), 1.0, 0.0).astype(bf16)
    lse_ref[0, :, :edge] = text_lse_ref[0, :, :edge]
    lse_ref[0, :, edge:] = text_lse_ref[0, :, edge:] + sum(dot_tn(piece, tall_spots) for piece in split_three(spread))

    scores = dot_nn(k_few, qkv_ref[:width, :]) + jnp.where(its_row < MEM, log_two, -1e9)
    scores = scores.reshape(HEADS, AUG, ROWS)
    text_lse = lse_ref[0, :HEADS, :]
    peak = jnp.maximum(text_lse, jnp.max(scores, axis=1))
    expo = jnp.exp(scores - peak[:, None, :])
    text_part = jnp.exp(text_lse - peak)
    total = text_part + jnp.sum(expo, axis=1)
    inverse = 1.0 / total
    lse_ref[0, :HEADS, :] = peak + jnp.log(total)
    text_part = text_part * inverse
    expo = (expo * inverse[:, None, :]).reshape(HEADS * AUG, ROWS).astype(bf16)
    extra = dot_tn(v_few, expo)
    for head in range(HEADS):
        rows = slice(head * HD, (head + 1) * HD)
        share = text_part[head : head + 1, :]
        mixed_ref[rows, :edge] = (mean_ref[rows, :edge].astype(f32) * share[:, :edge] + extra[rows, :edge]).astype(bf16)
        mixed_ref[rows, edge:] = (mean_edge[rows, :] * share[:, edge:] + extra[rows, edge:]).astype(bf16)

    first = z_ref[...] + (dot_tn(mixed_ref[...], attn_ref[3 * width :, :]) + vec_ref[2:3, :])
    normed, inverse = norm_rows(first)
    n1_ref[...] = normed.astype(bf16)
    r1_ref[...] = inverse
    h = normed * vec_ref[3:4, :] + vec_ref[4:5, :]
    h_ref[...] = h
    hl_ref[...] = h.astype(bf16)

    @pl.when(seg == 0)
    def _():
        wait_loads(weights, sems, 1)
        wait_loads(weights, sems, 2)

    blocks, block = bin_ref.shape
    for low in range(0, ROWS, ROWS // 2):
        rs = slice(low, low + ROWS // 2)
        for f in range(blocks):
            sl, cs = slice(f * width, (f + 1) * width), slice(f * block, (f + 1) * block)
            pre = dot_nn(hl_ref[rs, :], win_ref[sl, :]) + bin_ref[f : f + 1, :]
            act, slope = gelu_both(pre)
            act_ref[rs, cs] = act.astype(bf16)
            slope_ref[rs, cs] = slope.astype(bf16)
        part = dot_nt(act_ref[rs, :block], wout_ref[:width, :])
        for f in range(1, blocks):
            part += dot_nt(act_ref[rs, f * block : (f + 1) * block], wout_ref[f * width : (f + 1) * width, :])
        acc_ref[rs, :] = part

    normed, inverse = norm_rows(h_ref[...] + (acc_ref[...] + vec_ref[5:6, :]))
    n2_ref[...] = normed.astype(bf16)
    r2_ref[...] = inverse
    y = normed * vec_ref[6:7, :] + vec_ref[7:8, :]
    row = lax.broadcasted_iota(jnp.int32, (TEXT, 1), 0)
    out_ref[0] = jnp.where(row < limit, y[:TEXT, :], 0.0).astype(bf16)
    memory[:MEM, :] = jnp.where(seg < count, y[TEXT:, :], memory[:MEM, :])
    mem_ref[...] = memory[:MEM, :]


def backward_kernel(
    plan, n_pieces, count_ref, fill_ref, table_ref, grad_ref, mgrad_ref, vec_ref, *refs,
):
    pieces, refs = refs[:n_pieces], refs[n_pieces:]
    backward_segment(plan, pieces, count_ref, fill_ref, table_ref, grad_ref, mgrad_ref, vec_ref, *refs)


def backward_segment(
    plan, pieces, count_ref, fill_ref, table_ref, grad_ref, mgrad_ref, vec_ref,
    qkv_ref, mixed_ref, lse_ref, n1_ref, r1_ref, slope_ref, n2_ref, r2_ref,
    first_ref, gbranch_ref, gpre_ref, gattn_ref, gqkv_ref, vgrad_ref, bgrad_ref, gmem_ref,
    edge_ref, gm_ref, gy_ref, second_ref, acc_ref, mix_ref, cols_ref, attn_ref, win_ref, wout_ref, sems,
):
    weights = (attn_ref, win_ref, wout_ref)
    step = pl.program_id(0)
    seg = SEGS_MAX - 1 - step
    count, fill = count_ref[0], fill_ref[0]
    limit = fill_limit(seg, count, fill)
    width = gy_ref.shape[1]

    @pl.when(step == 0)
    def _():
        start_loads(table_ref, pieces, plan, weights, sems, (1, 2))
        gm_ref[...] = mgrad_ref[0]
        vgrad_ref[...] = jnp.zeros_like(vgrad_ref)
        bgrad_ref[...] = jnp.zeros_like(bgrad_ref)

    row = lax.broadcasted_iota(jnp.int32, (TEXT, 1), 0)
    gy_ref[:TEXT, :] = jnp.where(row < limit, grad_ref[0].astype(f32), 0.0)
    gy_ref[TEXT:, :] = jnp.where(seg < count, gm_ref[...], 0.0)

    def column_sum(value):
        return jnp.sum(value, axis=0, keepdims=True)

    gy = gy_ref[...]
    normed = n2_ref[...].astype(f32)
    vgrad_ref[6:7, :] += column_sum(gy * normed)
    vgrad_ref[7:8, :] += column_sum(gy)
    second = norm_rows_back(gy, normed, r2_ref[...], vec_ref[6:7, :])
    second_ref[...] = second
    gbranch_ref[...] = second.astype(bf16)
    vgrad_ref[5:6, :] += column_sum(gbranch_ref[...].astype(f32))

    @pl.when(step == 0)
    def _():
        wait_loads(weights, sems, 2)
        wait_loads(weights, sems, 1)
        start_loads(table_ref, pieces, plan, weights, sems, (0,))

    blocks, block = bgrad_ref.shape
    for f in range(blocks):
        sl = slice(f * block, (f + 1) * block)
        rows = slice(f * width, (f + 1) * width)
        hidden = dot_nn(gbranch_ref[...], wout_ref[rows, :])
        pre = (hidden * slope_ref[:, sl].astype(f32)).astype(bf16)
        gpre_ref[:, sl] = pre
        bgrad_ref[f : f + 1, :] += column_sum(pre.astype(f32))
        part = dot_nt(gpre_ref[:, sl], win_ref[rows, :])
        if f == 0:
            acc_ref[...] = part
        else:
            acc_ref[...] += part

    gh = second_ref[...] + acc_ref[...]
    normed = n1_ref[...].astype(f32)
    vgrad_ref[3:4, :] += column_sum(gh * normed)
    vgrad_ref[4:5, :] += column_sum(gh)
    first = norm_rows_back(gh, normed, r1_ref[...], vec_ref[3:4, :])
    second_ref[...] = first
    gattn_ref[...] = first.astype(bf16)
    vgrad_ref[2:3, :] += column_sum(gattn_ref[...].astype(f32))

    @pl.when(step == 0)
    def _():
        wait_loads(weights, sems, 0)

    mix_ref[...] = dot_nt(attn_ref[3 * width :, :], gattn_ref[...]).astype(bf16)

    ones = ones_three(ROWS)
    key_aug = aug_rows(key_bias(limit), ones)
    value_aug = aug_rows(ones, ())

    def maps_of(head):
        lo = head * HD
        q_h = qkv_ref[lo : lo + HD, :]
        k_h = qkv_ref[width + lo : width + lo + HD, :]
        v_h = qkv_ref[2 * width + lo : 2 * width + lo + HD, :]
        g_h = mix_ref[lo : lo + HD, :]
        inner = column_sum(g_h.astype(f32) * mixed_ref[lo : lo + HD, :].astype(f32))
        q_aug = jnp.concatenate([q_h, aug_rows(ones, split_three(-lse_ref[0, head : head + 1, :]))], axis=0)
        k_aug = jnp.concatenate([k_h, key_aug], axis=0)
        v_aug = jnp.concatenate([v_h, value_aug], axis=0)
        g_aug = jnp.concatenate([g_h, aug_rows(split_three(-inner), ())], axis=0)
        return dot_tn(q_aug, k_aug), dot_tn(g_aug, v_aug)

    def spread(head, grads, probs):
        lo = head * HD
        cols_ref[lo : lo + HD, :] = dot_nt(qkv_ref[width + lo : width + lo + HD, :], grads) * (HD ** (-0.5))
        cols_ref[width + lo : width + lo + HD, :] = dot_nn(qkv_ref[lo : lo + HD, :], grads)
        cols_ref[2 * width + lo : 2 * width + lo + HD, :] = dot_nn(mix_ref[lo : lo + HD, :], probs)

    maps = maps_of(0)
    for head in range(HEADS):
        following = maps_of(head + 1) if head + 1 < HEADS else None
        probs = jnp.exp(maps[0])
        spread(head, (probs * maps[1]).astype(bf16), probs.astype(bf16))
        maps = following

    for c in range(3):
        gqkv_ref[:, c * width : (c + 1) * width] = cols_ref[c * width : (c + 1) * width, :].T.astype(bf16)
    vgrad_ref[0:1, :] += column_sum(gqkv_ref[:, :width].astype(f32))
    vgrad_ref[1:2, :] += column_sum(gqkv_ref[:, 2 * width :].astype(f32))
    first_ref[...] = second_ref[...]
    edge = ROWS - AUG
    joined = second_ref[edge:, :]
    for c in range(3):
        joined = joined + dot_nt(gqkv_ref[edge:, c * width : (c + 1) * width], attn_ref[c * width : (c + 1) * width, :])
    edge_ref[...] = joined
    gm_ref[...] = jnp.where(seg < count, edge_ref[AUG - MEM :, :], gm_ref[...])
    gmem_ref[...] = gm_ref[...]


def whole():
    return pl.BlockSpec(memory_space=pltpu.VMEM)


def scalar():
    return pl.BlockSpec(memory_space=pltpu.SMEM)


def remain():
    return pl.BlockSpec(memory_space=pl.ANY)


def weight_scratch(width, blocks, block):
    return [
        pltpu.VMEM((4 * width, width), bf16), pltpu.VMEM((blocks * width, block), bf16),
        pltpu.VMEM((blocks * width, block), bf16),
    ]


def forward_call(count, fill, text, bias, vec, early, table, plan, pieces):
    width = text.shape[-1]
    blocks, block = bias.shape
    hidden = blocks * block
    total = SEGS_MAX * ROWS

    def rows(cols):
        return pl.BlockSpec((ROWS, cols), lambda s: (s, 0))

    def lanes(height):
        return pl.BlockSpec((height, ROWS), lambda s: (0, s))

    seg_block = pl.BlockSpec((1, TEXT, width), lambda s: (s, 0, 0))
    sds = jax.ShapeDtypeStruct
    return pl.pallas_call(
        functools.partial(forward_kernel, plan, len(pieces)),
        grid=(SEGS_MAX,),
        in_specs=[scalar(), scalar(), scalar(), seg_block] + [whole()] * 2
        + [lanes(3 * width), lanes(width), pl.BlockSpec((1, 16, ROWS), lambda s: (s, 0, 0))]
        + [remain()] * len(pieces),
        out_specs=[
            seg_block, pl.BlockSpec((MEM, width), lambda s: (0, 0)),
            rows(width), lanes(3 * width), lanes(width),
            pl.BlockSpec((1, 16, ROWS), lambda s: (s, 0, 0)),
            rows(width), rows(1), rows(width), rows(hidden), rows(hidden), rows(width), rows(1),
        ],
        out_shape=[
            sds((SEGS_MAX, TEXT, width), bf16), sds((MEM, width), f32),
            sds((total, width), bf16), sds((3 * width, total), bf16), sds((width, total), bf16),
            sds((SEGS_MAX, 16, ROWS), f32),
            sds((total, width), bf16), sds((total, 1), f32), sds((total, width), bf16),
            sds((total, hidden), bf16), sds((total, hidden), bf16), sds((total, width), bf16),
            sds((total, 1), f32),
        ],
        scratch_shapes=[
            pltpu.VMEM((AUG, width), f32), pltpu.VMEM((ROWS, width), f32),
            pltpu.VMEM((ROWS, width), f32), pltpu.VMEM((ROWS, width), f32),
        ]
        + weight_scratch(width, blocks, block)
        + [pltpu.SemaphoreType.DMA((3,))],
        compiler_params=pltpu.CompilerParams(vmem_limit_bytes=62 * 2**20),
    )(count, fill, table, text, bias, vec, *early, *pieces)


def backward_call(count, fill, out_grad, mem_grad, vec, saved, shape, table, plan, pieces):
    width = out_grad.shape[-1]
    blocks, block = shape
    hidden = blocks * block
    total = SEGS_MAX * ROWS
    last = SEGS_MAX - 1

    def rows(cols):
        return pl.BlockSpec((ROWS, cols), lambda s: (last - s, 0))

    def lanes(height):
        return pl.BlockSpec((height, ROWS), lambda s: (0, last - s))

    def fixed(*shape):
        return pl.BlockSpec(shape, lambda s: (0,) * len(shape))

    seg_block = pl.BlockSpec((1, TEXT, width), lambda s: (last - s, 0, 0))
    sds = jax.ShapeDtypeStruct
    return pl.pallas_call(
        functools.partial(backward_kernel, plan, len(pieces)),
        grid=(SEGS_MAX,),
        in_specs=[scalar(), scalar(), scalar(), seg_block] + [whole()] * 2 + [remain()] * len(pieces)
        + [
            lanes(3 * width), lanes(width), pl.BlockSpec((1, 16, ROWS), lambda s: (last - s, 0, 0)),
            rows(width), rows(1), rows(hidden), rows(width), rows(1),
        ],
        out_specs=[
            rows(width), rows(width), rows(hidden), rows(width), rows(3 * width),
            fixed(8, width), fixed(blocks, block), fixed(MEM, width),
        ],
        out_shape=[
            sds((total, width), f32), sds((total, width), bf16), sds((total, hidden), bf16),
            sds((total, width), bf16), sds((total, 3 * width), bf16),
            sds((8, width), f32), sds((blocks, block), f32), sds((MEM, width), f32),
        ],
        scratch_shapes=[
            pltpu.VMEM((AUG, width), f32), pltpu.VMEM((MEM, width), f32), pltpu.VMEM((ROWS, width), f32),
            pltpu.VMEM((ROWS, width), f32), pltpu.VMEM((ROWS, width), f32),
            pltpu.VMEM((width, ROWS), bf16), pltpu.VMEM((3 * width, ROWS), f32),
        ]
        + weight_scratch(width, blocks, block)
        + [pltpu.SemaphoreType.DMA((3,))],
        compiler_params=pltpu.CompilerParams(vmem_limit_bytes=62 * 2**20),
    )(count, fill, table, out_grad, mem_grad, vec, *pieces, *saved)


class Products:
    def __init__(self, jobs, block, own, small=None, plan=None, n_pieces=0):
        self.jobs, self.block, self.own, self.small, self.plan, self.n_pieces = jobs, block, own, small, plan, n_pieces
        self.loads = []
        for _, loads, _ in jobs:
            self.loads += [load for load in loads if load not in self.loads]

    def part(self, array, load):
        kind = load[1]
        if kind is None:
            return array.shape
        if kind[0] == "rows":
            return (ROWS, array.shape[1])
        return (array.shape[0], self.block)

    def kernel(self, n_in, n_out, index_ref, table_ref, *refs):
        n_loads, n_jobs = len(self.loads), len(self.jobs)
        inputs, refs = refs[:n_in], refs[n_in:]
        pieces, refs = refs[: self.n_pieces], refs[self.n_pieces :]
        outputs, refs = refs[:n_out], refs[n_out:]
        held, refs = refs[:n_loads], refs[n_loads:]
        results, refs = refs[:n_jobs], refs[n_jobs:]
        load_sem, store_sem, partial = refs[:3]
        weights, weight_sem = refs[3:4], refs[4:]
        step = pl.program_id(0)

        def load(n):
            source, kind = self.loads[n]
            view = inputs[source]
            if kind is not None:
                if kind[0] == "rows":
                    view = view.at[pl.ds(kind[1] * ROWS, ROWS), :]
                else:
                    place = index_ref[kind[1]] if kind[0] == "index" else kind[1]
                    view = view.at[:, pl.ds(pl.multiple_of(place * self.block, 128), self.block)]
            return pltpu.make_async_copy(view, held[n], load_sem.at[n])

        def half(n, part):
            source, kind = self.loads[n]
            rows = held[n].shape[0] // 2
            view = inputs[source].at[pl.ds(part * rows, rows), :]
            if kind is not None:
                place = index_ref[kind[1]] if kind[0] == "index" else kind[1]
                view = inputs[source].at[pl.ds(part * rows, rows), pl.ds(pl.multiple_of(place * self.block, 128), self.block)]
            return pltpu.make_async_copy(view, held[n].at[pl.ds(part * rows, rows), :], load_sem.at[n if part else n_loads + n])

        needs = [[self.loads.index(x) for x in loads] for _, loads, _ in self.jobs]
        fresh, seen = [], set()
        for need in needs:
            fresh.append([n for n in need if n not in seen])
            seen.update(need)

        def stores(n):
            kind, place, number = self.jobs[n][2]
            result, base = results[n], sum(self.store_counts[:n])
            if kind == "block":
                moves = [(result, outputs[place].at[number])]
            elif kind == "text":
                moves = []
            elif kind == "packed":
                moves = [(result, outputs[place].at[number])]
            else:
                mine, moves = index_ref[0], []
                for j in range(result.shape[0] // 2):
                    moves.append((result.at[2 * j + 1 - mine], outputs[place + 1].at[number, j]))
                    moves.append((result.at[2 * j + mine], outputs[place].at[number, j]))
            return [pltpu.make_async_copy(x, y, store_sem.at[base + m]) for m, (x, y) in enumerate(moves)]

        def shared_rows(n):
            extra = self.small[2]
            ffn = index_ref[self.jobs[n][1][1][1][1]]
            shard = results[n].shape[1] - extra
            return pltpu.make_async_copy(inputs[-1].at[:, ffn], results[n].at[:, pl.ds(shard, extra), :], store_sem.at[sum(self.store_counts) + n])

        for n, (form, _, output) in enumerate(self.jobs):

            @pl.when(step == n)
            def _():
                if n == 0:
                    for m in fresh[0]:
                        half(m, 0).start()
                if output[0] == "packed":
                    shared_rows(n).start()
                for m in fresh[n]:
                    (load(m) if n else half(m, 0)).wait()
                if n == 0:
                    for m in fresh[0]:
                        half(m, 1).start()
                else:
                    for m in fresh[n + 2] if n + 2 < n_jobs else ():
                        load(m).start()
                texts = [m for m, job in enumerate(self.jobs) if job[0] == "text"]
                if texts and n == texts[0] - 1:
                    start_loads(table_ref, pieces, self.plan, weights, weight_sem[0], (0,))
                if texts and n == texts[0]:
                    wait_loads(weights, weight_sem[0], 0)

            if n == 0:

                @pl.when(step == 0)
                def _():
                    rows = held[0].shape[0] // 2
                    partial[...] = dot_tn(held[needs[0][0]][:rows, :], held[needs[0][1]][:rows, :])

                @pl.when(step == 0)
                def _():
                    for m in fresh[0]:
                        half(m, 1).wait()
                    for m in sum(fresh[1:3], []):
                        load(m).start()

            @pl.when(step == n)
            def _():
                if form == "text":
                    seg = output[2]
                    width = weights[0].shape[1]
                    joined = held[needs[n][0]][...]
                    for c in range(3):
                        rows = held[needs[n][1 + c]][seg * ROWS : (seg + 1) * ROWS, :]
                        joined = joined + dot_nt(rows, weights[0][c * width : (c + 1) * width, :])
                    results[n][...] = joined
                    outputs[output[1]][0] = results[n][:TEXT, :]
                else:
                    left, right = needs[n]
                    if n == 0:
                        rows = held[left].shape[0] // 2
                        value = partial[...] + dot_tn(held[left][rows:, :], held[right][rows:, :])
                    else:
                        value = {"tn": dot_tn, "nn": dot_nn}[form](held[left][...], held[right][...])
                    value = value.astype(bf16)
                    if output[0] == "packed":
                        items, rows, _ = results[n].shape
                        shard = rows - self.small[2]
                        results[n][:, :shard, :] = value.reshape(items, shard, self.block)
                        shared_rows(n).wait()
                    else:
                        results[n][...] = value.reshape(results[n].shape)

            @pl.when(step == n)
            def _():
                for copy in stores(n):
                    copy.start()
                if n == n_jobs - 1:
                    for m in range(n_jobs):
                        for copy in stores(m):
                            copy.wait()

    def __call__(self, index, arrays, out_shapes, table=None, pieces=()):
        block, own = self.block, self.own
        width = block
        scratch = [pltpu.VMEM(self.part(arrays[x[0]], x), arrays[x[0]].dtype) for x in self.loads]
        self.store_counts = []
        for form, loads, (kind, _, _) in self.jobs:
            if kind == "text":
                scratch.append(pltpu.VMEM((ROWS, width), f32))
            elif kind == "packed":
                items, _, extra, _ = self.small
                scratch.append(pltpu.VMEM((items, width // items + extra, block), bf16))
            else:
                scratch.append(pltpu.VMEM((width // own, own, block) if kind == "split" else (width, block), bf16))
            self.store_counts.append({"split": width // own, "text": 0}.get(kind, 1))
        scratch += [
            pltpu.SemaphoreType.DMA((2 * len(self.loads),)),
            pltpu.SemaphoreType.DMA((sum(self.store_counts) + len(self.jobs),)),
            pltpu.VMEM((width, block), f32),
        ]
        if pieces:
            scratch += [pltpu.VMEM((4 * width, width), bf16), pltpu.SemaphoreType.DMA((1,))]
        ahead = len(self.jobs) - SEGS_MAX
        text_block = pl.BlockSpec((1, TEXT, width), lambda j: (jnp.maximum(j - ahead, 0), 0, 0))
        return pl.pallas_call(
            functools.partial(self.kernel, len(arrays), len(out_shapes)),
            grid=(len(self.jobs),),
            in_specs=[scalar(), scalar()] + [remain()] * (len(arrays) + len(pieces)),
            out_specs=[remain() if dtype == bf16 else text_block for _, dtype in out_shapes],
            out_shape=[jax.ShapeDtypeStruct(shape, dtype) for shape, dtype in out_shapes],
            scratch_shapes=scratch,
            compiler_params=pltpu.CompilerParams(vmem_limit_bytes=62 * 2**20),
        )(index, index if table is None else table, *arrays, *pieces)


def text_grad_kernel(plan, n_pieces, table_ref, first_ref, gqkv_ref, *refs):
    pieces = refs[:n_pieces]
    out_ref, joined_ref, attn_ref, sems = refs[n_pieces:]
    width = attn_ref.shape[1]

    @pl.when(pl.program_id(0) == 0)
    def _():
        start_loads(table_ref, pieces, plan, (attn_ref,), sems, (0,))
        wait_loads((attn_ref,), sems, 0)

    joined = first_ref[...]
    for c in range(3):
        joined = joined + dot_nt(gqkv_ref[:, c * width : (c + 1) * width], attn_ref[c * width : (c + 1) * width, :])
    joined_ref[...] = joined
    out_ref[0] = joined_ref[:TEXT, :]


def text_grad_call(first, gqkv, table, plan, pieces):
    width = first.shape[1]

    def rows(cols):
        return pl.BlockSpec((ROWS, cols), lambda s: (s, 0))

    return pl.pallas_call(
        functools.partial(text_grad_kernel, plan, len(pieces)),
        grid=(SEGS_MAX,),
        in_specs=[scalar(), rows(width), rows(3 * width)] + [remain()] * len(pieces),
        out_specs=pl.BlockSpec((1, TEXT, width), lambda s: (s, 0, 0)),
        out_shape=jax.ShapeDtypeStruct((SEGS_MAX, TEXT, width), f32),
        scratch_shapes=[
            pltpu.VMEM((ROWS, width), f32), pltpu.VMEM((4 * width, width), bf16), pltpu.SemaphoreType.DMA((1,)),
        ],
        compiler_params=pltpu.CompilerParams(vmem_limit_bytes=62 * 2**20),
    )(table, first, gqkv, *pieces)


def deal_kernel(outputs, places, n_in, n_out, index_ref, *refs):
    inputs, refs = refs[:n_in], refs[n_in:]
    outs, refs = refs[:n_out], refs[n_out:]
    load_sem, store_sem = refs[-2:]
    held = list(refs[:-2])
    results = held[-len(outputs) :]

    def view(array, indices):
        found = []
        for index in indices:
            if index is None:
                found.append(slice(None))
            elif isinstance(index, int):
                found.append(index)
            elif index[0] == "at":
                found.append(index_ref[index[1]] + index[2])
            else:
                found.append(pl.ds(index[0], index[1] - index[0]))
        return inputs[array].at[tuple(found)]

    waits, number = [], 0
    for _, views in outputs:
        waits.append([])
        for item in views:
            target, sem = held[number], load_sem.at[number]
            number += 1
            one = pltpu.make_async_copy(view(*item[:2]), target, sem)
            if len(item) == 2:
                one.start()
            else:
                (other, which) = item[2:]
                two = pltpu.make_async_copy(view(*other), target, sem)
                pl.when(index_ref[which] == 0)(one.start)
                pl.when(index_ref[which] != 0)(two.start)
            waits[-1].append((one, target))
    stores = []
    for n, items in enumerate(waits):
        total = None
        for copy, target in items:
            copy.wait()
            part = target[...].astype(f32)
            total = part if total is None else total + part
        results[n][...] = total.astype(bf16)
        out, first = places[n]
        target = outs[out] if first is None else outs[out].at[pl.ds(first, results[n].shape[0]), :]
        stores.append(pltpu.make_async_copy(results[n], target, store_sem.at[n]))
        stores[-1].start()
    for copy in stores:
        copy.wait()


def deal(index, outputs):
    arrays, places, shapes, flat = [], [], [], []
    for n, output in enumerate(outputs):
        if isinstance(output, list):
            first = 0
            for part in output:
                places.append((n, first))
                first += part[0][0]
                flat.append(part)
            shapes.append((first,) + output[0][0][1:])
        else:
            places.append((n, None))
            flat.append(output)
            shapes.append(output[0])
    outputs = flat

    def place(array):
        for n, known in enumerate(arrays):
            if known is array:
                return n
        arrays.append(array)
        return len(arrays) - 1

    plain = []
    for shape, views in outputs:
        plain.append((shape, [
            (place(v[0]), v[1]) if len(v) == 2 else (place(v[0]), v[1], (place(v[2][0]), v[2][1]), v[3]) for v in views
        ]))
    scratch = [pltpu.VMEM(shape, bf16) for shape, views in plain for _ in views]
    n_loads = len(scratch)
    scratch += [pltpu.VMEM(shape, bf16) for shape, _ in plain]
    scratch += [pltpu.SemaphoreType.DMA((n_loads,)), pltpu.SemaphoreType.DMA((len(plain),))]
    return pl.pallas_call(
        functools.partial(deal_kernel, plain, places, len(arrays), len(shapes)),
        in_specs=[scalar()] + [remain()] * len(arrays),
        out_specs=[remain()] * len(shapes),
        out_shape=[jax.ShapeDtypeStruct(shape, bf16) for shape in shapes],
        scratch_shapes=scratch,
        compiler_params=pltpu.CompilerParams(vmem_limit_bytes=62 * 2**20),
    )(index, *arrays)


class Piece:
    MINE = {"t": 4, "y": 6}

    def __init__(self, halves):
        self.halves = halves
        self.shard = halves[0][0][0].shape[-2:]

    def views(self, half, chosen):
        out = []
        for array, names, first in self.halves[half]:
            at = []
            for name in names:
                if name in chosen:
                    at.append(chosen[name])
                elif name == "s":
                    at.append((first, first + 2))
                else:
                    at.append(None)
            out.append((array, tuple(at)))
        return out

    def plane(self, step):
        outputs, self.names = [], []
        for half, order in enumerate(PLANE):
            axis = order[step][0]
            chosen = {axis: ("at", self.MINE[axis] + 1, 0)}
            if step == 1:
                chosen[order[0][0]] = ("at", self.MINE[order[0][0]], 0)
            names = [n for n in self.halves[half][0][1] if n not in chosen]
            outputs.append((tuple(2 for _ in names) + self.shard, self.views(half, chosen)))
            self.names.append(names)
        return outputs

    def swap_plane(self, step, sends):
        self.arrived = [swap(x, order[step][0], 2, 1) for x, order in zip(sends, PLANE)]

    def take(self):
        for half, (value, names) in enumerate(zip(self.arrived, self.names)):
            self.halves[half] = self.halves[half] + [(value, names, 0)]

    def line(self):
        outputs = []
        for mask in range(4):
            views = []
            here = {"t": ("at", 4, 0), "y": ("at", 6, 0)}
            for (a, names, first), (b, other_names, other_first) in zip(*self.halves):
                def at(names, first):
                    return tuple(("at", 12 + mask, first) if n == "s" else here[n] for n in names)
                views.append((a, at(names, first), (b, at(other_names, other_first)), 8 + mask))
            outputs.append((self.shard, views))
        return outputs

    def total(self, kept, arrived):
        return sum(x.astype(f32) for x in [kept] + arrived)


def swap(value, axis, size, mask):
    return lax.ppermute(value, axis, [(i, i ^ mask) for i in range(size)])


def after(value, *others):
    return lax.optimization_barrier((value, others))[0]


def moved(coords, place, mask):
    return [c[:place] + (c[place] ^ mask,) + c[place + 1 :] for c in coords]


PLANE = ((("t", 1), ("y", 2)), (("y", 2), ("t", 1)))


def gather_line(shard, sizes, beside):
    parts = [swap(shard, "s", sizes["s"], m) for m in range(1, sizes["s"])]
    parts, beside = lax.optimization_barrier((parts, beside))
    parts = [shard] + parts
    half = sizes["s"] // 2
    return (jnp.concatenate(parts[:half]), jnp.concatenate(parts[half:])), beside


def gather_first(halves, sizes, beside):
    arrived = []
    for value, ((axis, _), _) in zip(halves, PLANE):
        arrived.append([swap(value, axis, sizes[axis], m) for m in range(1, sizes[axis])])
    arrived, beside = lax.optimization_barrier((arrived, beside))
    return tuple(jnp.concatenate([value] + more) for value, more in zip(halves, arrived)), beside


def gather_last(values, sizes):
    return tuple(
        tuple(swap(value, axis, sizes[axis], m) for m in range(1, sizes[axis]))
        for value, (_, (axis, _)) in zip(values, PLANE)
    )


def gather_core(first, last, sizes):
    out = []
    half = sizes["s"] // 2
    for number, (value, more, ((axis, place), (last_axis, last_place))) in enumerate(zip(first, last, PLANE)):
        coords = [(m, 0, 0, 0) for m in range(number * half, (number + 1) * half)]
        coords = sum((moved(coords, place, m) for m in range(sizes[axis])), [])
        out.append((value, coords))
        out += [(extra, moved(coords, last_place, m)) for m, extra in enumerate(more, 1)]
    return out + [
        (swap(value, "c", sizes["c"], m), moved(coords, 3, m))
        for m in range(1, sizes["c"])
        for value, coords in out
    ]


def pick(value, axis, index):
    return lax.dynamic_index_in_dim(value, index, axis, keepdims=False)


def body(sizes, text_rows, attn_weight, vectors, w_in, b_in, w_out, seg_count, last_fill, out_grad, mem_grad):
    width = text_rows.shape[-1]
    block = w_in.shape[1]
    n_s, n_t, n_y, n_c = (sizes[a] for a in "styc")
    n_ffn, n_items = n_y * n_c, n_s * n_t
    devices = n_ffn * n_items
    shard = width // n_items
    own = attn_weight.shape[0]
    me = {a: lax.axis_index(a) for a in "styc"}

    small = jnp.concatenate([vectors.reshape(-1), b_in.reshape(-1)])
    vec_size, small_size = vectors.size, small.size
    small_rows = -(-small_size // (width * 16)) * 16
    small = jnp.pad(small, (0, small_rows * width - small_size)).reshape(small_rows, width)
    direct = own % 16 == 0 and shard % 16 == 0 and (n_s, n_t, n_y, n_c) == (4, 2, 2, 2)

    def absolute(masks):
        return [me[a] ^ m for a, m in zip("styc", masks)]

    if direct:
        text = with_layout_constraint(text_rows[0], Layout((0, 1, 2)))
        grads = with_layout_constraint(out_grad[0], Layout((0, 1, 2)))
        line, text = gather_line(jnp.concatenate([attn_weight, small]), sizes, text)
        first, grads = gather_first(line, sizes, grads)
        text_rows, out_grad = text[None], grads[None]
        last = gather_last(first, sizes)
        feeds = lax.all_gather(jnp.concatenate([w_in, w_out.T]), ("s", "t", "y", "c"), axis=0, tiled=True)
        gathered = [gather_core(first, last, sizes)]
        plan, table, pieces, smalls = [], [], [], []
        for target, found in enumerate(gathered):
            for value, coords in found:
                each = value.shape[0] // len(coords)
                for j, masks in enumerate(coords):
                    s, t, y, c = absolute(masks)
                    item, ffn = s * n_t + t, y * n_c + c
                    if target == 0:
                        plan.append((len(pieces), j * each, own, 0))
                        table.append((item * n_ffn + ffn) * own)
                        smalls.append((item * n_ffn + ffn, value[j * each + own]))
                    else:
                        plan.append((len(pieces), j * each, shard, target))
                        table.append(ffn * width + item * shard)
                pieces.append(value)
        for device in range(devices):
            item, ffn = device // n_ffn, device % n_ffn
            for target in (1, 2):
                plan.append((len(pieces), (2 * device + target - 1) * shard, shard, target))
                table.append(jnp.int32(ffn * width + item * shard))
        pieces.append(feeds)
        place = jnp.stack([d for d, _ in smalls])
        rows = jnp.stack([row for _, row in smalls])
        rows = rows[jnp.argsort(place)][:, :small_size]
    else:
        def all_of(value):
            return lax.all_gather(value, ("s", "t", "y", "c"), axis=0)

        def by_block(value):
            parts = all_of(value).reshape(n_items, n_ffn, shard, block)
            return parts.transpose(1, 0, 2, 3).reshape(n_ffn * width, block)

        pieces = [all_of(attn_weight).reshape(-1, width), by_block(w_in), by_block(w_out.T)]
        plan = [(i, 0, p.shape[0], i) for i, p in enumerate(pieces)]
        table = [jnp.int32(0)] * 3
        rows = all_of(small).reshape(devices, -1)[:, :small_size]
    table = jnp.stack(table).astype(jnp.int32)
    rows = rows.astype(f32)
    vec = rows[:, :vec_size].reshape(devices, vectors.shape[0], -1).transpose(1, 0, 2).reshape(-1, width)
    bias = rows[:, vec_size:].reshape(n_items, n_ffn, -1).transpose(1, 0, 2).reshape(n_ffn, block)
    col = vec[:2].T

    attn_plan = [entry for entry in plan if entry[3] == 0]
    attn_used = sorted({entry[0] for entry in attn_plan})
    attn_plan = [(attn_used.index(entry[0]),) + entry[1:] for entry in attn_plan]
    attn_pieces = [pieces[n] for n in attn_used]
    early = early_call(seg_count, last_fill, text_rows[0], col, table, attn_plan, attn_pieces)

    (activations, memory, zl, qkv, mixed, lse, n1, r1, hl, act, slope, n2, r2) = forward_call(
        seg_count, last_fill, text_rows[0], bias, vec, early, table, plan, pieces
    )
    first_grad, gbranch, gpre, gattn, gqkv, vgrad, bgrad, gmem = backward_call(
        seg_count, last_fill, out_grad[0], mem_grad, vec,
        (qkv, mixed, lse, n1, r1, slope, n2, r2), (n_ffn, block), table, plan, pieces,
    )

    n_vec = vectors.shape[0]

    small_total = jnp.concatenate([vgrad, gmem])

    if direct:
        mine = me["c"].astype(jnp.int32)
        index = jnp.stack([mine] + [n_c * y + mine for y in range(n_y)] + [n_c * y + 1 - mine for y in range(n_y)])

        def blocks_of(left, right, which, output, kind="block"):
            return [
                ("tn", ((left, None), (right, ("index", 1 + which * n_y + y))), (kind, output, y)) for y in range(n_y)
            ]

        plain = ((n_y, width, block), bf16)
        packed = ((n_y, n_items, shard + 16, block), bf16)
        dealt = [((4, width // own // 2, own, width), bf16)] * 2

        (out_send,) = Products(blocks_of(0, 1, 1, 0), block, own)(index, (gbranch, act), [plain])
        out_arrived = swap(out_send, "c", n_c, 1)
        small = jnp.concatenate(
            [
                small_total.reshape(n_vec, devices, -1).transpose(1, 0, 2).reshape(devices, -1),
                bgrad.reshape(n_ffn, n_items, -1).transpose(1, 0, 2).reshape(devices, -1),
            ],
            axis=1,
        ).astype(bf16)
        small = jnp.pad(small, ((0, 0), (0, 16 * block - small_size))).reshape(n_items, n_ffn, 16, block)
        out_keep, in_send = Products(
            blocks_of(0, 1, 0, 0) + blocks_of(2, 3, 1, 1, "packed"), block, own, small.shape
        )(index, (after(gbranch, out_send), act, hl, gpre, small), [plain, packed])

        def shaped(value):
            return value.reshape(n_y, n_s, n_t, -1, block)

        def attn_shaped(value):
            return value.reshape(n_s, n_t, n_y, own, width)

        out_arrived, out_keep, in_send = lax.optimization_barrier((out_arrived, out_keep, in_send))
        lines = [me["s"] ^ m for m in range(4)]
        grid_index = jnp.stack(
            lines + [me["t"], me["t"] ^ 1, me["y"], me["y"] ^ 1] + [x // 2 for x in lines] + [x % 2 for x in lines]
        ).astype(jnp.int32)

        def deal_all(*groups):
            found, out = deal(grid_index, sum(groups, [])), []
            for group in groups:
                out.append(found[: len(group)])
                found = found[len(group) :]
            return out

        out = Piece([[(shaped(x), "yst", 2 * n) for x in (out_keep, out_arrived)] for n in range(2)])
        (sends,) = deal_all(out.plane(0))
        out.swap_plane(0, sends)
        in_arrived = swap(in_send, "c", n_c, 1)
        in_keep, attn_keep, attn_send = Products(
            blocks_of(0, 1, 0, 0, "packed")
            + [("tn", ((2, None), (3, ("column", c))), ("split", 1, c)) for c in range(3)]
            + [("nn", ((4, None), (5, None)), ("split", 1, 3))],
            block, own, small.shape,
        )(index, (after(hl, sends), gpre, zl, gqkv, mixed, gattn, small), [packed] + dealt)
        out.arrived, in_arrived, in_keep, attn_keep, attn_send = lax.optimization_barrier(
            (out.arrived, in_arrived, in_keep, attn_keep, attn_send)
        )

        out.take()
        feed = Piece([[(shaped(x), "yst", 2 * n) for x in (in_keep, in_arrived)] for n in range(2)])
        sends, more = deal_all(out.plane(1), feed.plane(0))
        out.swap_plane(1, sends)
        feed.swap_plane(0, more)
        attn_arrived = swap(attn_send, "c", n_c, 1)
        text_grad = text_grad_call(after(first_grad, sends, more), gqkv, table, attn_plan, attn_pieces)
        out.arrived, feed.arrived, attn_arrived, text_grad = lax.optimization_barrier(
            (out.arrived, feed.arrived, attn_arrived, text_grad)
        )

        out.take()
        feed.take()
        last = Piece([[(attn_shaped(x), "sty", 2 * n) for x in (attn_keep, attn_arrived)] for n in range(2)])
        out_line = out.line()
        more, lasts, (out_kept, out_two) = deal_all(feed.plane(1), last.plane(0), [out_line[0], out_line[2]])
        last.swap_plane(0, lasts)
        feed.swap_plane(1, more)
        out_two = swap(out_two, "s", 4, 2)
        text_grad = with_layout_constraint(after(text_grad, more).transpose(1, 0, 2), Layout((0, 1, 2)))
        out_two, feed.arrived, last.arrived, text_grad = lax.optimization_barrier(
            (out_two, feed.arrived, last.arrived, text_grad)
        )

        feed.take()
        last.take()
        in_line = feed.line()
        more, (in_kept, in_two, one, three) = deal_all(
            last.plane(1), [in_line[0], in_line[2], [out_line[1], in_line[1]], [out_line[3], in_line[3]]]
        )
        last.swap_plane(1, more)
        one, three, in_two = swap(one, "s", 4, 1), swap(three, "s", 4, 3), swap(in_two, "s", 4, 2)
        activations = with_layout_constraint(after(activations, more).transpose(1, 0, 2), Layout((0, 1, 2)))
        one, three, in_two, last.arrived, activations = lax.optimization_barrier(
            (one, three, in_two, last.arrived, activations)
        )

        last.take()
        attn_kept, *lines = deal_all(last.line())[0]
        lines = [swap(part, "s", 4, m) for m, part in enumerate(lines, 1)]
        w_out_grad = out.total(out_kept, [one[:shard], out_two, three[:shard]]).T
        in_own = feed.total(in_kept, [one[shard:], in_two, three[shard:]])
        w_in_grad = in_own[:shard]
        small_own = in_own[shard:].reshape(-1)[:small_size]
        vector_grad = small_own[:vec_size].reshape(vectors.shape)
        b_in_grad = small_own[vec_size:].reshape(b_in.shape)
        attn_grad = last.total(attn_kept, lines)
        activations, text_grad = activations.transpose(1, 0, 2), text_grad.transpose(1, 0, 2)
    else:
        axes = ("s", "t", "y", "c")

        def scatter_block(left, right):
            total = dot_tn(left, right).astype(bf16).reshape(n_items, shard, n_ffn, block).transpose(0, 2, 1, 3)
            total = total.reshape(devices, shard, block)
            return lax.psum_scatter(total, axes, scatter_dimension=0, tiled=False).astype(f32)

        w_out_grad = scatter_block(gbranch, act).T
        w_in_grad = scatter_block(hl, gpre)
        total = [dot_tn(zl, gqkv[:, c * width : (c + 1) * width]) for c in range(3)] + [dot_nn(mixed, gattn)]
        total = jnp.concatenate(total).astype(bf16)
        attn_grad = lax.psum_scatter(total, axes, scatter_dimension=0, tiled=True).astype(f32)
        vector_grad = lax.psum_scatter(small_total, axes, scatter_dimension=1, tiled=True)
        b_total = bgrad.reshape(n_ffn, n_items, -1).transpose(1, 0, 2).reshape(devices, 1, -1)
        b_in_grad = lax.psum_scatter(b_total, axes, scatter_dimension=0, tiled=False)
        text_grad = text_grad_call(first_grad, gqkv, table, attn_plan, attn_pieces)
    return (activations[None], memory[None], text_grad[None], attn_grad, vector_grad, w_in_grad, b_in_grad, w_out_grad)


def solution(mesh):
    items, ffn = mesh.shape["items"], mesh.shape["ffn"]
    sizes = {"s": 4, "t": items // 4, "y": ffn // 2, "c": 2}
    grid = jax.sharding.Mesh(mesh.devices.reshape(tuple(sizes.values())), tuple(sizes))
    both, item, feed = P(("s", "t", "y", "c")), ("s", "t"), ("y", "c")
    last = P(None, ("s", "t", "y", "c"))
    return jax.shard_map(
        functools.partial(body, sizes),
        mesh=grid,
        in_specs=(both, both, last, P(item, feed), P(feed, item), P(feed, item), both, both, both, both),
        out_specs=(both, both, both, both, last, P(item, feed), P(feed, item), P(feed, item)),
        check_vma=False,
    )
```
